512 devices in a mesh: batch: 8 (over x, y_lo), ctx: 64 (over y_hi, z, core).
Axes of the slice: x: 4, y: 4 (y_hi: 2, y_lo: 2; y = y_hi * 2 + y_lo), z: 16, core: 2. Of those that a mesh axis runs over, the one named last changes fastest.
Arguments:
- queries: bfloat16 [8, 16384, 768], P('batch', 'ctx'), may hold values from -8 to 8
- keys: bfloat16 [8, 16384, 768], P('batch', 'ctx'), may hold values from -8 to 8
- values: bfloat16 [8, 16384, 768], P('batch', 'ctx'), may hold values from -6 to 6
- cotangent: bfloat16 [8, 16384, 768], P('batch', 'ctx'), may hold values from -6 to 6
- out_weight: bfloat16 [768, 768], replicated, may hold values from -0.21875 to 0.21875
- offsets: int32 [16], replicated, may hold values from 0 to 15, each once
Outputs:
- grad_queries: bfloat16 [8, 16384, 768], P('batch', 'ctx')
- grad_keys: bfloat16 [8, 16384, 768], P('batch', 'ctx')
- grad_values: bfloat16 [8, 16384, 768], P('batch', 'ctx')
- grad_out_weight: float32 [768, 768], P('ctx', 'batch')
The draws below stay inside these ranges and needn't reach their ends.
All inputs are finite; a program needn't handle non-finite values.
Results may differ from the reference program's by a relative error of at most 0.035.
Values may be sent and summed in bfloat16 or wider, within the bound.
No kernel may reach another device: no remote copies, remote signals or barrier semaphores. Data moves between devices by JAX's collectives and lax.ppermute only.
A program may use at most 64 MiB of HBM per device.

```python
import math
import jax
import jax.numpy as jnp
from jax import lax

D = 768
H = 16
LEVELS = 4
SEGS = 64
SLIDES = 8
TOKENS = 16384


def draw_queries(key, part):
    own_key = jax.random.fold_in(key, 7)
    result = jax.random.truncated_normal(own_key, -6.0, 6.0, (SLIDES, TOKENS, D), jnp.float32)
    return result.astype(jnp.bfloat16)


def draw_keys(key, part):
    own_key = jax.random.fold_in(key, 8)
    result = jax.random.truncated_normal(own_key, -6.0, 6.0, (SLIDES, TOKENS, D), jnp.float32)
    return result.astype(jnp.bfloat16)


def block_scale(rng, extent, pieces, smallest, top_value):
    gain, own = 1.0, jax.random.fold_in(rng, 6)
    for position, blocks in pieces:
        steps = jnp.exp(jax.random.uniform(jax.random.fold_in(own, position), (blocks,), jnp.float32, smallest / len(pieces), top_value / len(pieces)))
        gain = gain * jnp.repeat(steps, extent[position] // blocks).reshape([-1 if axis == position else 1 for axis in range(len(extent))])
    return gain


def gaussian(key, extent, spread, limit, pieces=(), dtype=jnp.bfloat16):
    values = spread * jax.random.normal(key, extent, jnp.float32)
    if pieces:
        values = values * block_scale(key, extent, pieces, -0.22, 0.18)
    return jnp.clip(values, -limit, limit).astype(dtype)


def setup_inputs(seed: int = 0) -> dict:
    streams_of = jax.random.split(jax.random.key(seed), 7)
    queries = draw_queries(jax.random.fold_in(streams_of[6], 71), 0)
    keys = draw_keys(jax.random.fold_in(streams_of[6], 71), 0)
    values = gaussian(streams_of[2], (SLIDES, TOKENS, D), 1.0, 6.0, ((0, 8), (1, 64)))
    cotangent = gaussian(streams_of[3], (SLIDES, TOKENS, D), 1.0, 6.0, ((0, 8), (1, 64)))
    out_weight = gaussian(streams_of[4], (D, D), D ** -0.5, 0.21875)
    offsets = jax.random.permutation(streams_of[5], H).astype(jnp.int32)
    return dict(queries=queries, keys=keys, values=values, cotangent=cotangent, out_weight=out_weight, offsets=offsets)


def reference(queries, keys, values, cotangent, out_weight, offsets):
    head_width = D // H
    group_heads = H // LEVELS
    seg_keys = TOKENS // SEGS
    softmax_scale = 1.0 / math.sqrt(head_width)

    def one_slide(slide_arrays):
        query_rows, key_rows, value_rows, grad_rows = slide_arrays
        grad_attended = jnp.dot(grad_rows, out_weight.T, preferred_element_type=jnp.float32).astype(jnp.bfloat16)
        grad_attended = lax.optimization_barrier(grad_attended)
        attended_parts = []
        query_parts = []
        key_parts = []
        value_parts = []
        for head_index in range(H):
            dilation = 2 ** (head_index // group_heads)
            head_offset = (offsets[head_index] % dilation).astype(jnp.int32)
            first_col = head_index * head_width
            stacked = TOKENS // dilation

            def select_rows(matrix):
                rows_form = matrix[:, first_col:first_col + head_width].reshape(stacked, dilation, head_width)
                chosen = lax.dynamic_index_in_dim(rows_form, head_offset, 1, keepdims=False)
                return chosen.reshape(SEGS // dilation, seg_keys, head_width).astype(jnp.float32)

            def place_rows(segment_form, dtype_out):
                rows_form = segment_form.reshape(stacked, 1, head_width).astype(dtype_out)
                empty_rows = jnp.zeros((stacked, dilation, head_width), dtype_out)
                filled = lax.dynamic_update_slice_in_dim(empty_rows, rows_form, head_offset, 1)
                return filled.reshape(TOKENS, head_width)
            query_sel = select_rows(query_rows)
            key_sel = select_rows(key_rows)
            value_sel = select_rows(value_rows)
            grad_sel = select_rows(grad_attended)
            scores = jnp.einsum('sqd,skd->sqk', query_sel, key_sel) * softmax_scale
            top_score = lax.optimization_barrier(jnp.max(scores, axis=-1, keepdims=True))
            log_total = top_score + jnp.log(lax.optimization_barrier(jnp.sum(jnp.exp(scores - top_score), axis=-1, keepdims=True)))
            weights = jnp.exp(scores - log_total)
            weights_low = lax.optimization_barrier(weights.astype(jnp.bfloat16)).astype(jnp.float32)
            attended = jnp.einsum('sqk,skd->sqd', weights_low, value_sel).astype(jnp.bfloat16)
            attended_wide = lax.optimization_barrier(attended).astype(jnp.float32)
            row_dots = lax.optimization_barrier(jnp.sum(grad_sel * attended_wide, axis=-1, keepdims=True))
            grad_weights = jnp.einsum('sqd,skd->sqk', grad_sel, value_sel)
            grad_scores = weights * (grad_weights - row_dots)
            grad_scores = lax.optimization_barrier(grad_scores.astype(jnp.bfloat16)).astype(jnp.float32)
            grad_query = jnp.einsum('sqk,skd->sqd', grad_scores, key_sel) * softmax_scale
            grad_key = jnp.einsum('sqk,sqd->skd', grad_scores, query_sel) * softmax_scale
            grad_value = jnp.einsum('sqk,sqd->skd', weights_low, grad_sel)
            attended_parts.append(place_rows(attended, jnp.bfloat16))
            query_parts.append(place_rows(grad_query, jnp.float32))
            key_parts.append(place_rows(grad_key, jnp.float32))
            value_parts.append(place_rows(grad_value, jnp.float32))
        attended_all = jnp.concatenate(attended_parts, axis=1)
        weight_term = jnp.dot(attended_all.T, grad_rows, preferred_element_type=jnp.float32)
        grad_q = jnp.concatenate(query_parts, axis=1).astype(jnp.bfloat16)
        grad_k = jnp.concatenate(key_parts, axis=1).astype(jnp.bfloat16)
        grad_v = jnp.concatenate(value_parts, axis=1).astype(jnp.bfloat16)
        return (grad_q, grad_k, grad_v, weight_term)
    grad_q, grad_k, grad_v, weight_terms = lax.map(one_slide, (queries, keys, values, cotangent))
    return (grad_q, grad_k, grad_v, lax.optimization_barrier(jnp.sum(weight_terms, axis=0)))
```

```python
import functools
import math

import jax
import jax.numpy as jnp
from jax import lax
from jax.experimental import pallas as pl
from jax.experimental.pallas import tpu as pltpu
from jax.sharding import PartitionSpec as P

LEVELS = 4
HEADS = 16
HEAD_WIDTH = 48
PAIR_WIDTH = 2 * HEAD_WIDTH
LEVEL_WIDTH = 4 * HEAD_WIDTH
LANES = 128
ROWS = 256
MODEL = 768
SCALE = 1.0 / math.sqrt(HEAD_WIDTH)
BF = jnp.bfloat16
F32 = jnp.float32
VMEM_LIMIT = 48 * 1024 * 1024


def groups_over(bits, count):
    found = {}
    for index in range(count):
        rest = index
        for bit in bits:
            rest &= ~(1 << bit)
        found.setdefault(rest, []).append(index)
    return list(found.values())


def mm(a, b):
    return jnp.dot(a, b, preferred_element_type=F32)


def mm_nt(a, b):
    return lax.dot_general(a, b, (((1,), (1,)), ((), ())), preferred_element_type=F32)


def mm_tn(a, b):
    return lax.dot_general(a, b, (((0,), (0,)), ((), ())), preferred_element_type=F32)


def iota(shape, dim):
    return lax.broadcasted_iota(jnp.int32, shape, dim)


def one_hot(condition):
    return jnp.where(condition, 1.0, 0.0).astype(BF)


def first_head(shape):
    return (iota(shape, 1) & (LANES - 1)) < HEAD_WIDTH


def pack_kernel(off_ref, q_ref, k_ref, v_ref, c_ref, w_ref, near_ref, four_ref, eight_ref, wide):
    wide[...] = jnp.zeros_like(wide)
    grad = mm_nt(c_ref[...], w_ref[...]).astype(BF)
    for half in range(2):
        for level in range(LEVELS):
            start = LEVEL_WIDTH * level + PAIR_WIDTH * half
            for place, rows in enumerate((q_ref[...], k_ref[...], v_ref[...], grad)):
                wide[half, level, :, LANES * place : LANES * place + PAIR_WIDTH] = rows[
                    :, start : start + PAIR_WIDTH
                ]
    for half in range(2):
        near_ref[half, 0:ROWS, :] = wide[half, 0]
        for level in range(1, LEVELS):
            dilation = 1 << level
            count = ROWS // dilation
            source = wide[half, level]
            target = iota((count, ROWS), 1) - dilation * iota((count, ROWS), 0)
            picked = []
            for head in range(2):
                offset = off_ref[4 * level + 2 * half + head] & (dilation - 1)
                picked.append(mm(one_hot(target == offset), source))
            chosen = jnp.where(first_head(picked[0].shape), picked[0], picked[1]).astype(BF)
            if level == 1:
                near_ref[half, ROWS : ROWS + count, :] = chosen
            elif level == 2:
                four_ref[half] = chosen
                four_ref[half + 2] = chosen
            else:
                for chip in range(4):
                    eight_ref[half + 2 * chip] = chosen


def attend(packed):
    q, k, v, g = (packed[:, LANES * i : LANES * (i + 1)] for i in range(4))
    lane = iota(q.shape, 1)
    zero = jnp.zeros((), BF)
    total = [None] * 4
    for head in range(2):
        own = (lane >= HEAD_WIDTH * head) & (lane < HEAD_WIDTH * (head + 1))
        qh, kh, vh, gh = (jnp.where(own, part, zero) for part in (q, k, v, g))
        scores = mm_nt(q, kh) * SCALE
        top = jnp.max(scores, axis=1, keepdims=True)
        raw = jnp.exp(scores - top)
        weights = raw * (1.0 / jnp.sum(raw, axis=1, keepdims=True))
        low = weights.astype(BF)
        attended = mm(low, vh).astype(BF)
        row_dots = jnp.sum(gh.astype(F32) * attended.astype(F32), axis=1, keepdims=True)
        grad_scores = (weights * (mm_nt(g, vh) - row_dots)).astype(BF)
        parts = (
            attended,
            (mm(grad_scores, kh) * SCALE).astype(BF),
            (mm_tn(grad_scores, qh) * SCALE).astype(BF),
            mm_tn(low, gh).astype(BF),
        )
        total = [new if old is None else old + new for old, new in zip(total, parts)]
    return jnp.concatenate(total, axis=1)


def attention_kernel(off_ref, near_ref, four_ref, eight_ref, c_ref, weight_ref, grads_ref):
    position = lax.axis_index("ctx")
    half = position & 1
    chip = position >> 1
    folded = None
    for level in range(LEVELS):
        dilation = 1 << level
        if level == 0:
            placed = jnp.concatenate([attend(near_ref[core, 0:ROWS, :]) for core in range(2)], axis=0)
        else:
            if level == 1:
                packed = jnp.concatenate([near_ref[core, ROWS:, :] for core in range(2)], axis=0)
            elif level == 2:
                packed = four_ref[...].reshape(ROWS, 4 * LANES)
            else:
                packed = eight_ref[...].reshape(ROWS, 4 * LANES)
            done = attend(packed)
            first_row = (chip & (dilation // 2 - 1)) * (2 * ROWS)
            shape = (2 * ROWS, ROWS)
            target = iota(shape, 0) - dilation * iota(shape, 1) + first_row
            spread = []
            for head in range(2):
                offset = off_ref[4 * level + 2 * half + head] & (dilation - 1)
                spread.append(mm(one_hot(target == offset), done))
            placed = jnp.where(first_head(spread[0].shape), spread[0], spread[1]).astype(BF)
        shape = (LANES, LEVELS * PAIR_WIDTH)
        fold = one_hot(iota(shape, 1) == jnp.where(iota(shape, 0) < PAIR_WIDTH, iota(shape, 0) + PAIR_WIDTH * level, -1))
        part = mm(placed[:, 0:LANES], fold)
        folded = part if folded is None else folded + part
        for core in range(2):
            for array in range(3):
                lanes = LEVELS * LANES * array + LANES * level
                grads_ref[core, :, lanes : lanes + LANES] = placed[
                    ROWS * core : ROWS * (core + 1), LANES * (array + 1) : LANES * (array + 2)
                ]
    weight_ref[...] = mm_tn(c_ref[...], folded.astype(BF)).astype(BF)


def merge_kernel(grads_ref, dq_ref, dk_ref, dv_ref):
    for array, out_ref in enumerate((dq_ref, dk_ref, dv_ref)):
        for level in range(LEVELS):
            lanes = LEVELS * LANES * array + LANES * level
            for half in range(2):
                start = LEVEL_WIDTH * level + PAIR_WIDTH * half
                out_ref[:, start : start + PAIR_WIDTH] = grads_ref[half, :, lanes : lanes + PAIR_WIDTH]


def split_kernel(sums_ref, out_ref):
    core = lax.axis_index("ctx") & 1
    shape = (512, LEVELS * PAIR_WIDTH)
    row = iota(shape, 0)
    column = iota(shape, 1)
    inner = row & 15
    source = 24 * (row >> 4) + 12 * core + inner
    level = (source >= 192).astype(jnp.int32) + (source >= 384).astype(jnp.int32) + (source >= 576).astype(jnp.int32)
    rest = source - LEVEL_WIDTH * level
    second = rest >= PAIR_WIDTH
    wanted = PAIR_WIDTH * level + jnp.where(second, rest - PAIR_WIDTH, rest)
    hit = (column == wanted) & (inner < 12)
    out = mm_nt(one_hot(hit & ~second), sums_ref[0]) + mm_nt(one_hot(hit & second), sums_ref[1])
    out_ref[...] = out.astype(BF)


def call(kernel, out_shape, *operands, scalars=0, scratch=()):
    vmem = pl.BlockSpec(memory_space=pltpu.VMEM)
    smem = pl.BlockSpec(memory_space=pltpu.SMEM)
    return pl.pallas_call(
        kernel,
        out_shape=out_shape,
        in_specs=[smem] * scalars + [vmem] * (len(operands) - scalars),
        out_specs=jax.tree.map(lambda _: vmem, out_shape),
        scratch_shapes=list(scratch),
        compiler_params=pltpu.CompilerParams(vmem_limit_bytes=VMEM_LIMIT),
    )(*operands)


def exchange(block, bits):
    return lax.all_to_all(block, "ctx", 0, 0, tiled=True, axis_index_groups=groups_over(bits, 64))


def local(queries, keys, values, cotangent, out_weight, offsets):
    def bf(*shape):
        return jax.ShapeDtypeStruct(shape, BF)

    near, four, eight = call(
        pack_kernel,
        (bf(2, 384, 512), bf(4, 64, 512), bf(8, 32, 512)),
        offsets, queries[0], keys[0], values[0], cotangent[0], out_weight,
        scalars=1,
        scratch=(pltpu.VMEM((2, LEVELS, ROWS, 4 * LANES), BF),),
    )
    near = exchange(near, (0,))
    four = exchange(four, (0, 1))
    eight = exchange(eight, (0, 1, 2))
    both = lax.all_gather(cotangent[0], "ctx", axis=0, tiled=True, axis_index_groups=groups_over((0,), 64))
    weight_part, grads = call(
        attention_kernel,
        (bf(MODEL, 384), bf(2, ROWS, 3 * 512)),
        offsets, near, four, eight, both,
        scalars=1,
    )
    column_parts = lax.all_to_all(weight_part.reshape(8, 96, 384), "batch", 0, 0, tiled=True)
    column_sum = jnp.sum(column_parts.astype(F32), axis=0).astype(BF)
    sums = lax.all_gather(column_sum, "ctx", axis=0, tiled=False, axis_index_groups=groups_over((0,), 64))
    row_parts = call(split_kernel, bf(512, 96), sums)
    row_parts = exchange(row_parts.reshape(32, 16, 96), (1, 2, 3, 4, 5))
    weight_grad = jnp.sum(row_parts.astype(F32), axis=0)[:12]
    grads = exchange(grads, (0,))
    dq, dk, dv = call(merge_kernel, (bf(ROWS, MODEL),) * 3, grads)
    return dq[None], dk[None], dv[None], weight_grad


def solution(mesh):
    rows = P("batch", "ctx", None)
    return jax.shard_map(
        local,
        mesh=mesh,
        in_specs=(rows, rows, rows, rows, P(), P()),
        out_specs=(rows, rows, rows, P("ctx", "batch")),
        check_vma=False,
    )
```

```python
import math

import jax
import jax.numpy as jnp
from jax import lax
from jax.experimental import pallas as pl
from jax.experimental.pallas import tpu as pltpu
from jax.sharding import PartitionSpec as P

LEVELS = 4
HEADS = 16
HEAD_WIDTH = 48
PAIR_WIDTH = 2 * HEAD_WIDTH
LEVEL_WIDTH = 4 * HEAD_WIDTH
LANES = 128
ROWS = 256
MODEL = 768
HALF_LANES = 6 * LANES
SCALE = 1.0 / math.sqrt(HEAD_WIDTH)
BF = jnp.bfloat16
F32 = jnp.float32
VMEM_LIMIT = 24 * 1024 * 1024


def groups_over(bits, count):
    found = {}
    for index in range(count):
        rest = index
        for bit in bits:
            rest &= ~(1 << bit)
        found.setdefault(rest, []).append(index)
    return list(found.values())


def mm(a, b):
    return jnp.dot(a, b, preferred_element_type=F32)


def mm_nt(a, b):
    return lax.dot_general(a, b, (((1,), (1,)), ((), ())), preferred_element_type=F32)


def mm_tn(a, b):
    return lax.dot_general(a, b, (((0,), (0,)), ((), ())), preferred_element_type=F32)


def iota(shape, dim):
    return lax.broadcasted_iota(jnp.int32, shape, dim)


def one_hot(condition):
    return jnp.where(condition, 1.0, 0.0).astype(BF)


def first_head(shape):
    return (iota(shape, 1) & (LANES - 1)) < HEAD_WIDTH


def pack_kernel(
    off_ref, q_hbm, k_hbm, v_hbm, c_hbm, w_hbm, mine_ref, other_ref, four_ref, eight_ref, wide, q_ref, k_ref, v_ref, c_ref, w_ref, sems
):
    moves = start_all(((c_hbm, c_ref), (w_hbm, w_ref), (q_hbm, q_ref), (k_hbm, k_ref), (v_hbm, v_ref)), sems)
    core = lax.axis_index("ctx") & 1
    wide[...] = jnp.zeros_like(wide)
    moves[0].wait()
    cotangent = c_ref[...]
    half_rows = ROWS // 2
    other_ref[384:640, :] = cotangent[:, :512]
    other_ref[640:768, 0:256] = cotangent[:half_rows, 512:]
    other_ref[640:768, 256:512] = cotangent[half_rows:, 512:]
    moves[1].wait()
    grad = mm_nt(cotangent, w_ref[...]).astype(BF)
    for place, rows_ref in ((0, q_ref), (1, k_ref), (2, v_ref), (3, None)):
        if rows_ref is not None:
            moves[2 + place].wait()
        rows = grad if rows_ref is None else rows_ref[...]
        for half in range(2):
            for level in range(LEVELS):
                start = LEVEL_WIDTH * level + PAIR_WIDTH * half
                wide[half, level, :, LANES * place : LANES * place + PAIR_WIDTH] = rows[:, start : start + PAIR_WIDTH]
    for half in range(2):
        for level in range(1, LEVELS):
            dilation = 1 << level
            count = ROWS // dilation
            target = iota((count, ROWS), 1) - dilation * iota((count, ROWS), 0)
            hits = [
                one_hot(target == (off_ref[4 * level + 2 * half + head] & (dilation - 1))) for head in range(2)
            ]
            picked = mm(jnp.concatenate(hits, axis=0), wide[half, level])
            chosen = jnp.where(first_head((count, 4 * LANES)), picked[:count], picked[count:]).astype(BF)
            if level == 2:
                four_ref[half] = chosen
                four_ref[half + 2] = chosen
            elif level == 3:
                for chip in range(4):
                    eight_ref[half + 2 * chip] = chosen
            else:

                @pl.when(core == half)
                def _(chosen=chosen, half=half):
                    mine_ref[0:ROWS, :] = wide[half, 0]
                    mine_ref[ROWS:, :] = chosen

                @pl.when(core != half)
                def _(chosen=chosen, half=half):
                    other_ref[0:ROWS, :] = wide[half, 0]
                    other_ref[ROWS:384, :] = chosen


def attend(packed, backward=True):
    q, k, v, g = (packed[:, LANES * i : LANES * (i + 1)] for i in range(4))
    lane = iota(q.shape, 1)
    zero = jnp.zeros((), BF)
    total = None
    for head in range(2):
        own = (lane >= HEAD_WIDTH * head) & (lane < HEAD_WIDTH * (head + 1))
        qh, kh, vh, gh = (jnp.where(own, part, zero) for part in (q, k, v, g))
        scores = mm_nt(q, kh) * SCALE
        top = jnp.max(scores, axis=1, keepdims=True)
        raw = jnp.exp(scores - top)
        weights = raw * (1.0 / jnp.sum(raw, axis=1, keepdims=True))
        low = weights.astype(BF)
        attended = mm(low, vh).astype(BF)
        parts = [attended]
        if backward:
            row_dots = jnp.sum(gh.astype(F32) * attended.astype(F32), axis=1, keepdims=True)
            grad_scores = (weights * (mm_nt(g, vh) - row_dots)).astype(BF)
            parts += [
                (mm(grad_scores, kh) * SCALE).astype(BF),
                (mm_tn(grad_scores, qh) * SCALE).astype(BF),
                mm_tn(low, gh).astype(BF),
            ]
        total = parts if total is None else [old + new for old, new in zip(total, parts)]
    return jnp.concatenate(total, axis=1) if backward else total[0]


def place_rows(off_ref, done, level):
    position = lax.axis_index("ctx")
    core = position & 1
    chip = position >> 1
    dilation = 1 << level
    count = 2 * ROWS
    row = iota((count, ROWS), 0)
    target = row - dilation * iota((count, ROWS), 1)
    if level > 1:
        first_row = (chip & (dilation // 2 - 1)) * count
        target = (row ^ (ROWS * core)) - dilation * iota((count, ROWS), 1) + first_row
    hits = [one_hot(target == (off_ref[4 * level + 2 * core + head] & (dilation - 1))) for head in range(2)]
    spread = mm(jnp.concatenate(hits, axis=0), done)
    return jnp.where(first_head((count, done.shape[1])), spread[:count], spread[count:]).astype(BF)


def fold_lanes(rows, level):
    shape = (LANES, LEVELS * PAIR_WIDTH)
    lane = iota(shape, 0)
    return mm(rows, one_hot(iota(shape, 1) == jnp.where(lane < PAIR_WIDTH, lane + PAIR_WIDTH * level, -1)))


def grad_lanes(array, level):
    return LANES * (2 * array + level % 2)


def store_grads(keep_ref, send_ref, placed, level):
    for array in range(3):
        lanes = grad_lanes(array, level)
        part = placed[:, LANES * (array + 1) : LANES * (array + 2)]
        keep_ref[:, lanes : lanes + LANES] = part[:ROWS]
        send_ref[:, lanes : lanes + LANES] = part[ROWS:]


def start_all(pairs, sems):
    moves = [pltpu.make_async_copy(source, target, sems.at[index]) for index, (source, target) in enumerate(pairs)]
    for move in moves:
        move.start()
    return moves


def wait_all(moves):
    for move in moves:
        move.wait()


def near_segments(mine_ref, other_ref):
    return (
        mine_ref[0:ROWS, :],
        other_ref[0:ROWS, :],
        jnp.concatenate([mine_ref[ROWS:384, :], other_ref[ROWS:384, :]], axis=0),
    )


def near_attended_kernel(off_ref, mine_ref, other_ref, attended_ref):
    done = [attend(segment, backward=False) for segment in near_segments(mine_ref, other_ref)]
    folded = fold_lanes(jnp.concatenate(done[:2], axis=0), 0)
    folded += fold_lanes(place_rows(off_ref, done[2], 1), 1)
    attended_ref[...] = folded.astype(BF)


def near_grads_kernel(off_ref, mine_ref, other_ref, keep_hbm, send_hbm, keep_ref, send_ref, sems):
    done = [attend(segment) for segment in near_segments(mine_ref, other_ref)]
    store_grads(keep_ref, send_ref, jnp.concatenate(done[:2], axis=0), 0)
    store_grads(keep_ref, send_ref, place_rows(off_ref, done[2], 1), 1)
    wait_all(start_all(((keep_ref, keep_hbm), (send_ref, send_hbm)), sems))


def weight_kernel(off_ref, own_ref, other_ref, four_ref, eight_ref, attended_ref, weight_ref):
    folded = attended_ref[...]
    for level, segment_ref in ((2, four_ref), (3, eight_ref)):
        done = attend(segment_ref[...].reshape(ROWS, 4 * LANES), backward=False)
        folded += fold_lanes(place_rows(off_ref, done, level), level).astype(BF)
    narrow = jnp.concatenate([other_ref[640:768, 0:256], other_ref[640:768, 256:512]], axis=0)
    other = jnp.concatenate([other_ref[384:640, :], narrow], axis=1)
    part = mm_tn(jnp.concatenate([own_ref[...], other], axis=0), folded).astype(BF)
    for column in range(8):
        rows = part[96 * column : 96 * (column + 1)]
        weight_ref[2 * column, 0:96, :] = rows[:, 0:128]
        weight_ref[2 * column, 96:144, 0:64] = rows[0:48, 128:192]
        weight_ref[2 * column, 96:144, 64:128] = rows[48:96, 128:192]
        weight_ref[2 * column + 1, 0:96, :] = rows[:, 256:384]
        weight_ref[2 * column + 1, 96:144, 0:64] = rows[0:48, 192:256]
        weight_ref[2 * column + 1, 96:144, 64:128] = rows[48:96, 192:256]


def far_grads_kernel(off_ref, four_ref, eight_ref, keep_hbm, send_hbm, keep_ref, send_ref, sems):
    for level, segment_ref in ((2, four_ref), (3, eight_ref)):
        done = attend(segment_ref[...].reshape(ROWS, 4 * LANES))
        store_grads(keep_ref, send_ref, place_rows(off_ref, done, level), level)
    wait_all(start_all(((keep_ref, keep_hbm), (send_ref, send_hbm)), sems))


def merge_kernel(near_hbm, far_hbm, got_near_hbm, got_far_hbm, dq_hbm, dk_hbm, dv_hbm, keep_ref, got_ref, out_ref, sems):
    core = lax.axis_index("ctx") & 1
    wait_all(
        start_all(
            (
                (near_hbm, keep_ref.at[0]),
                (far_hbm, keep_ref.at[1]),
                (got_near_hbm.at[1 - core], got_ref.at[0]),
                (got_far_hbm.at[1 - core], got_ref.at[1]),
            ),
            sems,
        )
    )
    for own in range(2):

        @pl.when(core == own)
        def _(own=own):
            for array in range(3):
                for level in range(LEVELS):
                    lanes = grad_lanes(array, level)
                    for half in range(2):
                        source = keep_ref if half == own else got_ref
                        start = LEVEL_WIDTH * level + PAIR_WIDTH * half
                        out_ref[array, :, start : start + PAIR_WIDTH] = source[level // 2, :, lanes : lanes + PAIR_WIDTH]

    wait_all(start_all([(out_ref.at[array], out) for array, out in enumerate((dq_hbm, dk_hbm, dv_hbm))], sems))


def split_kernel(sums_ref, out_ref):
    position = lax.axis_index("ctx")
    core = position & 1
    upper = position >> 5
    shape = (256, LANES)
    row = iota(shape, 0)
    lane = iota(shape, 1)
    inner = row & 15
    source = 24 * (row >> 4) + 12 * core + inner
    second_level = (source >= LEVEL_WIDTH).astype(jnp.int32)
    rest = source - LEVEL_WIDTH * second_level
    second_half = rest >= PAIR_WIDTH
    column = PAIR_WIDTH * second_level + jnp.where(second_half, rest - PAIR_WIDTH, rest)
    wide_first = jnp.where(upper == 0, 0, 64)
    narrow_first = jnp.where(upper == 0, 128, 0)
    in_wide = (lane == column - wide_first) & (inner < 12)
    in_narrow = (lane == column - narrow_first) & (inner < 12)
    out = None
    for half in range(2):
        mine = second_half if half else ~second_half
        wide = one_hot(in_wide & mine)
        narrow = one_hot(in_narrow & mine & (lane < 64))
        sums = sums_ref[half]
        tail = sums[96:144]
        tail_rows = jnp.concatenate([tail, pltpu.roll(tail.astype(F32), 64, 1).astype(BF)], axis=0)
        part = mm_nt(wide, sums[0:96]) + mm_nt(narrow, tail_rows)
        out = part if out is None else out + part
    out_ref[:, 0:96] = out.astype(BF)
    out_ref[:, 96:128] = jnp.zeros((256, 32), BF)


def call(kernel, out_shape, *operands, smem=True, hbm=0, hbm_out=False, scratch=(), flops=0):
    vmem = pl.BlockSpec(memory_space=pltpu.VMEM)
    far = pl.BlockSpec(memory_space=pltpu.HBM)
    specs = [pl.BlockSpec(memory_space=pltpu.SMEM)] * smem
    specs += [vmem] * (len(operands) - smem - hbm) + [far] * hbm
    near = len(operands) - hbm
    operands = operands[:near] + tuple(pltpu.with_memory_space_constraint(x, pltpu.HBM) for x in operands[near:])
    return pl.pallas_call(
        kernel,
        out_shape=jax.tree.map(lambda x: pltpu.HBM(x.shape, x.dtype), out_shape) if hbm_out else out_shape,
        in_specs=specs,
        out_specs=jax.tree.map(lambda _: far if hbm_out else vmem, out_shape),
        scratch_shapes=list(scratch),
        compiler_params=pltpu.CompilerParams(vmem_limit_bytes=VMEM_LIMIT),
        cost_estimate=pl.CostEstimate(flops=flops, bytes_accessed=0, transcendentals=0) if flops else None,
    )(*operands)


def exchange(block, bits):
    return lax.all_to_all(block, "ctx", 0, 0, tiled=True, axis_index_groups=groups_over(bits, 64))


def pair_gather(block):
    return lax.all_gather(block, "ctx", axis=0, tiled=False, axis_index_groups=groups_over((0,), 64))


def swap(block):
    return lax.ppermute(block, "ctx", [(index, index ^ 1) for index in range(64)])


def local(queries, keys, values, cotangent, out_weight, offsets):
    def bf(*shape):
        return jax.ShapeDtypeStruct(shape, BF)

    def vmem(*shape):
        return pltpu.VMEM(shape, BF)

    def dma(count):
        return pltpu.SemaphoreType.DMA((count,))

    rows = vmem(ROWS, MODEL)
    mine, other, four, eight = call(
        pack_kernel,
        (bf(384, 512), bf(768, 512), bf(4, 64, 512), bf(8, 32, 512)),
        offsets, queries[0], keys[0], values[0], cotangent[0], out_weight,
        hbm=5,
        scratch=(vmem(2, LEVELS, ROWS, 4 * LANES), rows, rows, rows, rows, vmem(MODEL, MODEL), dma(5)),
    )
    other = swap(other)
    four = exchange(four, (0, 1))
    attended = call(near_attended_kernel, bf(2 * ROWS, 384), offsets, mine, other, flops=2_000_000_000)
    attended, eight = lax.optimization_barrier((attended, eight))
    eight = exchange(eight, (0, 1, 2))
    half = vmem(ROWS, HALF_LANES)
    grads = dict(hbm_out=True, scratch=(half, half, dma(2)), flops=5_000_000_000)
    near_keep, near_send = call(near_grads_kernel, (bf(ROWS, HALF_LANES),) * 2, offsets, mine, other, **grads)
    attended, near_send = lax.optimization_barrier((attended, near_send))
    weight_parts = call(
        weight_kernel, bf(16, 144, 128), offsets, cotangent[0], other, four, eight, attended, flops=2_000_000_000
    )
    weight_parts, four, eight = lax.optimization_barrier((weight_parts, four, eight))
    plane = [[64 * batch + 32 * top + rest for batch in range(8) for top in range(2)] for rest in range(32)]
    column_parts = lax.all_to_all(weight_parts, ("batch", "ctx"), 0, 0, tiled=True, axis_index_groups=plane)
    far_keep, far_send = call(far_grads_kernel, (bf(ROWS, HALF_LANES),) * 2, offsets, four, eight, **grads)
    column_sum = jnp.sum(column_parts.astype(F32), axis=0).astype(BF)
    row_parts = call(split_kernel, bf(256, 128), pair_gather(column_sum), smem=False)
    row_parts, near_send, far_send = lax.optimization_barrier((row_parts, near_send, far_send))
    row_parts = exchange(row_parts.reshape(16, 16, 128), (1, 2, 3, 4))
    weight_grad = jnp.sum(row_parts.astype(F32), axis=0)[:12, :96]
    both = vmem(2, ROWS, HALF_LANES)
    dq, dk, dv = call(
        merge_kernel,
        (bf(ROWS, MODEL),) * 3,
        near_keep, far_keep, pair_gather(near_send), pair_gather(far_send),
        smem=False, hbm=4, hbm_out=True, scratch=(both, both, vmem(3, ROWS, MODEL), dma(4)), flops=2_000_000_000,
    )
    return dq[None], dk[None], dv[None], weight_grad


def solution(mesh):
    rows = P("batch", "ctx", None)
    return jax.shard_map(
        local,
        mesh=mesh,
        in_specs=(rows, rows, rows, rows, P(), P()),
        out_specs=(rows, rows, rows, P("ctx", "batch")),
        check_vma=False,
    )
```

```python
import math

import jax
import jax.numpy as jnp
from jax import lax
from jax.experimental import pallas as pl
from jax.experimental.pallas import tpu as pltpu
from jax.sharding import PartitionSpec as P

LEVELS = 4
HEADS = 16
HEAD_WIDTH = 48
PAIR_WIDTH = 2 * HEAD_WIDTH
LEVEL_WIDTH = 4 * HEAD_WIDTH
LANES = 128
ROWS = 256
MODEL = 768
GRAD_LANES = 3 * LANES
SENT = 448
SCALE = 1.0 / math.sqrt(HEAD_WIDTH)
BF = jnp.bfloat16
F32 = jnp.float32
VMEM_LIMIT = 24 * 1024 * 1024


def groups_over(bits, count):
    found = {}
    for index in range(count):
        rest = index
        for bit in bits:
            rest &= ~(1 << bit)
        found.setdefault(rest, []).append(index)
    return list(found.values())


def mm(a, b):
    return jnp.dot(a, b, preferred_element_type=F32)


def mm_nt(a, b):
    return lax.dot_general(a, b, (((1,), (1,)), ((), ())), preferred_element_type=F32)


def mm_tn(a, b):
    return lax.dot_general(a, b, (((0,), (0,)), ((), ())), preferred_element_type=F32)


def iota(shape, dim):
    return lax.broadcasted_iota(jnp.int32, shape, dim)


def one_hot(condition):
    return jnp.where(condition, 1.0, 0.0).astype(BF)


def first_head(shape):
    return (iota(shape, 1) & (LANES - 1)) < HEAD_WIDTH


def pack_kernel(
    off_ref, q_hbm, k_hbm, v_hbm, c_hbm, w_hbm, mine_ref, other_ref, eight_ref, wide, q_ref, k_ref, v_ref, c_ref, w_ref, sems
):
    moves = start_all(((c_hbm, c_ref), (w_hbm, w_ref), (q_hbm, q_ref), (k_hbm, k_ref), (v_hbm, v_ref)), sems)
    core = lax.axis_index("ctx") & 1
    wide[...] = jnp.zeros_like(wide)
    moves[0].wait()
    cotangent = c_ref[...]
    half_rows = ROWS // 2
    other_ref[SENT:704, :] = cotangent[:, :512]
    other_ref[704:832, 0:256] = cotangent[:half_rows, 512:]
    other_ref[704:832, 256:512] = cotangent[half_rows:, 512:]
    moves[1].wait()
    grad = mm_nt(cotangent, w_ref[...]).astype(BF)
    for place, rows_ref in ((0, q_ref), (1, k_ref), (2, v_ref), (3, None)):
        if rows_ref is not None:
            moves[2 + place].wait()
        rows = grad if rows_ref is None else rows_ref[...]
        for half in range(2):
            for level in range(LEVELS):
                start = LEVEL_WIDTH * level + PAIR_WIDTH * half
                wide[half, level, :, LANES * place : LANES * place + PAIR_WIDTH] = rows[:, start : start + PAIR_WIDTH]
    for half in range(2):
        for level in range(1, LEVELS):
            dilation = 1 << level
            count = ROWS // dilation
            target = iota((count, ROWS), 1) - dilation * iota((count, ROWS), 0)
            hits = [
                one_hot(target == (off_ref[4 * level + 2 * half + head] & (dilation - 1))) for head in range(2)
            ]
            picked = mm(jnp.concatenate(hits, axis=0), wide[half, level])
            chosen = jnp.where(first_head((count, 4 * LANES)), picked[:count], picked[count:]).astype(BF)
            if level == 3:
                for chip in range(4):
                    eight_ref[half + 2 * chip] = chosen
            else:
                first = ROWS if level == 1 else 384

                @pl.when(core == half)
                def _(chosen=chosen, first=first, count=count):
                    mine_ref[first : first + count, :] = chosen

                @pl.when(core != half)
                def _(chosen=chosen, first=first, count=count):
                    other_ref[first : first + count, :] = chosen

        @pl.when(core == half)
        def _(half=half):
            mine_ref[0:ROWS, :] = wide[half, 0]

        @pl.when(core != half)
        def _(half=half):
            other_ref[0:ROWS, :] = wide[half, 0]


def attend(packed, backward=True):
    q, k, v, g = (packed[:, LANES * i : LANES * (i + 1)] for i in range(4))
    lane = iota(q.shape, 1)
    zero = jnp.zeros((), BF)
    total = None
    for head in range(2):
        own = (lane >= HEAD_WIDTH * head) & (lane < HEAD_WIDTH * (head + 1))
        qh, kh, vh, gh = (jnp.where(own, part, zero) for part in (q, k, v, g))
        scores = mm_nt(q, kh) * SCALE
        top = jnp.max(scores, axis=1, keepdims=True)
        raw = jnp.exp(scores - top)
        weights = raw * (1.0 / jnp.sum(raw, axis=1, keepdims=True))
        low = weights.astype(BF)
        attended = mm(low, vh).astype(BF)
        parts = [attended]
        if backward:
            row_dots = jnp.sum(gh.astype(F32) * attended.astype(F32), axis=1, keepdims=True)
            grad_scores = (weights * (mm_nt(g, vh) - row_dots)).astype(BF)
            parts += [
                (mm(grad_scores, kh) * SCALE).astype(BF),
                (mm_tn(grad_scores, qh) * SCALE).astype(BF),
                mm_tn(low, gh).astype(BF),
            ]
        total = parts if total is None else [old + new for old, new in zip(total, parts)]
    return jnp.concatenate(total, axis=1) if backward else total[0]


def place_rows(off_ref, done, level):
    position = lax.axis_index("ctx")
    core = position & 1
    dilation = 1 << level
    count = 2 * ROWS
    shape = (count, done.shape[0])
    row = iota(shape, 0)
    if level == 3:
        row = (row ^ (ROWS * core)) + ((position >> 1) & 3) * count
    target = row - dilation * iota(shape, 1)
    hits = [one_hot(target == (off_ref[4 * level + 2 * core + head] & (dilation - 1))) for head in range(2)]
    spread = mm(jnp.concatenate(hits, axis=0), done)
    return jnp.where(first_head((count, done.shape[1])), spread[:count], spread[count:]).astype(BF)


def fold_lanes(rows, level):
    shape = (LANES, LEVELS * PAIR_WIDTH)
    lane = iota(shape, 0)
    return mm(rows, one_hot(iota(shape, 1) == jnp.where(lane < PAIR_WIDTH, lane + PAIR_WIDTH * level, -1)))


def store_grads(target_ref, rows, place):
    target_ref[:, GRAD_LANES * place : GRAD_LANES * (place + 1)] = rows[:, LANES:]


def start_all(pairs, sems):
    moves = [pltpu.make_async_copy(source, target, sems.at[index]) for index, (source, target) in enumerate(pairs)]
    for move in moves:
        move.start()
    return moves


def wait_all(moves):
    for move in moves:
        move.wait()


def first_kernel(off_ref, mine_ref, other_ref, attended_ref, two_ref, keep_hbm, send_hbm, keep_ref, send_ref, sems):
    two_ref[0:64, :] = mine_ref[384:SENT, :]
    two_ref[64:128, :] = other_ref[384:SENT, :]
    packed = jnp.concatenate([mine_ref[ROWS:384, :], other_ref[ROWS:384, :]], axis=0)
    placed = place_rows(off_ref, attend(packed), 1)
    store_grads(keep_ref, placed[:ROWS], 0)
    store_grads(send_ref, placed[ROWS:], 0)
    moves = start_all(((keep_ref, keep_hbm), (send_ref, send_hbm)), sems)
    done = [attend(source[0:ROWS, :], backward=False) for source in (mine_ref, other_ref)]
    folded = fold_lanes(jnp.concatenate(done, axis=0), 0) + fold_lanes(placed[:, :LANES], 1)
    attended_ref[...] = folded.astype(BF)
    wait_all(moves)


def second_kernel(off_ref, eight_ref, old_ref, first_hbm, attended_ref, keep_hbm, send_hbm, keep_ref, send_ref, sems):
    first = start_all(((first_hbm, send_ref.at[:, pl.ds(0, GRAD_LANES)]),), sems)
    placed = place_rows(off_ref, attend(eight_ref[...].reshape(ROWS, 4 * LANES)), 3)
    store_grads(keep_ref, placed[:ROWS], 0)
    store_grads(send_ref, placed[ROWS:], 1)
    attended_ref[...] = old_ref[...] + fold_lanes(placed[:, :LANES], 3).astype(BF)
    wait_all(first)
    wait_all(start_all(((keep_ref, keep_hbm), (send_ref, send_hbm)), sems))


def weight_kernel(off_ref, own_ref, other_ref, two_ref, got_two_ref, attended_ref, weight_ref):
    done = attend(jnp.concatenate([two_ref[...], got_two_ref[...]], axis=0), backward=False)
    folded = attended_ref[...] + fold_lanes(place_rows(off_ref, done[:ROWS // 2], 2), 2).astype(BF)
    narrow = jnp.concatenate([other_ref[704:832, 0:256], other_ref[704:832, 256:512]], axis=0)
    other = jnp.concatenate([other_ref[SENT:704, :], narrow], axis=1)
    part = mm_tn(jnp.concatenate([own_ref[...], other], axis=0), folded).astype(BF)
    for column in range(8):
        rows = part[96 * column : 96 * (column + 1)]
        weight_ref[2 * column, 0:96, :] = rows[:, 0:128]
        weight_ref[2 * column, 96:144, 0:64] = rows[0:48, 128:192]
        weight_ref[2 * column, 96:144, 64:128] = rows[48:96, 128:192]
        weight_ref[2 * column + 1, 0:96, :] = rows[:, 256:384]
        weight_ref[2 * column + 1, 96:144, 0:64] = rows[0:48, 192:256]
        weight_ref[2 * column + 1, 96:144, 64:128] = rows[48:96, 192:256]


def last_kernel(off_ref, mine_ref, other_ref, two_ref, got_two_ref, keep_hbm, send_hbm, keep_ref, send_ref, sems):
    store_grads(keep_ref, attend(mine_ref[0:ROWS, :]), 0)
    store_grads(send_ref, attend(other_ref[0:ROWS, :]), 0)
    done = attend(jnp.concatenate([two_ref[...], got_two_ref[...]], axis=0))
    placed = place_rows(off_ref, done[: ROWS // 2], 2)
    store_grads(keep_ref, placed[:ROWS], 1)
    store_grads(send_ref, placed[ROWS:], 1)
    wait_all(start_all(((keep_ref, keep_hbm), (send_ref, send_hbm)), sems))


def merge_kernel(
    keep1_hbm, keep3_hbm, keep02_hbm, got13_hbm, got02_hbm, dq_hbm, dk_hbm, dv_hbm, keep_ref, got_ref, out_ref, sems
):
    core = lax.axis_index("ctx") & 1
    moves = start_all(
        (
            (keep1_hbm, keep_ref.at[:, pl.ds(GRAD_LANES, GRAD_LANES)]),
            (keep3_hbm, keep_ref.at[:, pl.ds(3 * GRAD_LANES, GRAD_LANES)]),
            (keep02_hbm.at[:, pl.ds(0, GRAD_LANES)], keep_ref.at[:, pl.ds(0, GRAD_LANES)]),
            (keep02_hbm.at[:, pl.ds(GRAD_LANES, GRAD_LANES)], keep_ref.at[:, pl.ds(2 * GRAD_LANES, GRAD_LANES)]),
            (got02_hbm.at[1 - core], got_ref.at[0]),
            (got13_hbm.at[1 - core], got_ref.at[1]),
        ),
        sems,
    )
    wait_all(moves)
    out_moves = []
    for array, out_hbm in enumerate((dq_hbm, dk_hbm, dv_hbm)):
        for own in range(2):

            @pl.when(core == own)
            def _(own=own, array=array):
                for level in range(LEVELS):
                    for half in range(2):
                        start = LEVEL_WIDTH * level + PAIR_WIDTH * half
                        if half == own:
                            lanes = GRAD_LANES * level + LANES * array
                            part = keep_ref[:, lanes : lanes + PAIR_WIDTH]
                        else:
                            lanes = GRAD_LANES * (level // 2) + LANES * array
                            part = got_ref[level % 2, :, lanes : lanes + PAIR_WIDTH]
                        out_ref[array, :, start : start + PAIR_WIDTH] = part

        out_moves.append(pltpu.make_async_copy(out_ref.at[array], out_hbm, sems.at[array]))
        out_moves[-1].start()
    wait_all(out_moves)


def split_kernel(sums_ref, out_ref):
    position = lax.axis_index("ctx")
    core = position & 1
    upper = position >> 5
    shape = (256, LANES)
    row = iota(shape, 0)
    lane = iota(shape, 1)
    inner = row & 15
    source = 24 * (row >> 4) + 12 * core + inner
    second_level = (source >= LEVEL_WIDTH).astype(jnp.int32)
    rest = source - LEVEL_WIDTH * second_level
    second_half = rest >= PAIR_WIDTH
    column = PAIR_WIDTH * second_level + jnp.where(second_half, rest - PAIR_WIDTH, rest)
    wide_first = jnp.where(upper == 0, 0, 64)
    narrow_first = jnp.where(upper == 0, 128, 0)
    in_wide = (lane == column - wide_first) & (inner < 12)
    in_narrow = (lane == column - narrow_first) & (inner < 12)
    out = None
    for half in range(2):
        mine = second_half if half else ~second_half
        wide = one_hot(in_wide & mine)
        narrow = one_hot(in_narrow & mine & (lane < 64))
        sums = sums_ref[half]
        tail = sums[96:144]
        tail_rows = jnp.concatenate([tail, pltpu.roll(tail.astype(F32), 64, 1).astype(BF)], axis=0)
        part = mm_nt(wide, sums[0:96]) + mm_nt(narrow, tail_rows)
        out = part if out is None else out + part
    out_ref[:, 0:96] = out.astype(BF)
    out_ref[:, 96:128] = jnp.zeros((256, 32), BF)


def call(kernel, out_shape, *operands, smem=True, hbm=0, hbm_out=(), scratch=(), flops=0):
    vmem = pl.BlockSpec(memory_space=pltpu.VMEM)
    far = pl.BlockSpec(memory_space=pltpu.HBM)
    specs = [pl.BlockSpec(memory_space=pltpu.SMEM)] * smem
    specs += [vmem] * (len(operands) - smem - hbm) + [far] * hbm
    near = len(operands) - hbm
    operands = operands[:near] + tuple(pltpu.with_memory_space_constraint(x, pltpu.HBM) for x in operands[near:])
    out_specs = vmem
    if isinstance(out_shape, tuple):
        out_shape, out_specs = list(out_shape), [vmem] * len(out_shape)
        for index in hbm_out:
            out_shape[index] = pltpu.HBM(out_shape[index].shape, out_shape[index].dtype)
            out_specs[index] = far
    return pl.pallas_call(
        kernel,
        out_shape=out_shape,
        in_specs=specs,
        out_specs=out_specs,
        scratch_shapes=list(scratch),
        compiler_params=pltpu.CompilerParams(vmem_limit_bytes=VMEM_LIMIT),
        cost_estimate=pl.CostEstimate(flops=flops, bytes_accessed=0, transcendentals=0) if flops else None,
    )(*operands)


def pair_gather(block):
    return lax.all_gather(block, "ctx", axis=0, tiled=False, axis_index_groups=groups_over((0,), 64))


def swap(block, bit):
    return lax.ppermute(block, "ctx", [(index, index ^ (1 << bit)) for index in range(64)])


def local(queries, keys, values, cotangent, out_weight, offsets):
    def bf(*shape):
        return jax.ShapeDtypeStruct(shape, BF)

    def vmem(*shape):
        return pltpu.VMEM(shape, BF)

    def dma(count):
        return pltpu.SemaphoreType.DMA((count,))

    rows = vmem(ROWS, MODEL)
    mine, other, eight = call(
        pack_kernel,
        (bf(SENT, 512), bf(832, 512), bf(8, 32, 512)),
        offsets, queries[0], keys[0], values[0], cotangent[0], out_weight,
        hbm=5,
        scratch=(vmem(2, LEVELS, ROWS, 4 * LANES), rows, rows, rows, rows, vmem(MODEL, MODEL), dma(5)),
    )
    eight = lax.all_to_all(eight, "ctx", 0, 0, tiled=True, axis_index_groups=groups_over((0, 1, 2), 64))
    other = swap(other, 0)

    def grads(*widths):
        return dict(
            hbm_out=tuple(range(-len(widths), 0)),
            scratch=tuple(vmem(ROWS, width) for width in widths) + (dma(2),),
            flops=5_000_000_000,
        )

    one, two = GRAD_LANES, 2 * GRAD_LANES
    attended, own_two, keep1, send1 = call(
        first_kernel,
        (bf(2 * ROWS, 384), bf(128, 512), bf(ROWS, one), bf(ROWS, one)),
        offsets, mine, other,
        **grads(one, one),
    )
    got_two = swap(own_two, 1)
    attended, keep3, send13 = call(
        second_kernel,
        (bf(2 * ROWS, 384), bf(ROWS, one), bf(ROWS, two)),
        offsets, eight, attended, send1,
        hbm=1, **grads(one, two),
    )
    weight_parts = call(
        weight_kernel,
        bf(16, 144, 128),
        offsets, cotangent[0], other, own_two, got_two, attended,
        flops=2_000_000_000,
    )
    weight_parts, mine, other, send13 = lax.optimization_barrier((weight_parts, mine, other, send13))
    plane = [[64 * batch + 32 * top + rest for batch in range(8) for top in range(2)] for rest in range(32)]
    column_parts = lax.all_to_all(weight_parts, ("batch", "ctx"), 0, 0, tiled=True, axis_index_groups=plane)
    keep02, send02 = call(
        last_kernel, (bf(ROWS, two), bf(ROWS, two)), offsets, mine, other, own_two, got_two, **grads(two, two)
    )
    column_parts, got13 = lax.optimization_barrier((column_parts, pair_gather(send13)))
    column_sum = jnp.sum(column_parts.astype(F32), axis=0).astype(BF)
    row_parts = call(split_kernel, bf(256, 128), pair_gather(column_sum), smem=False)
    row_parts, send02 = lax.optimization_barrier((row_parts, send02))
    row_parts = lax.all_to_all(
        row_parts.reshape(16, 16, 128), "ctx", 0, 0, tiled=True, axis_index_groups=groups_over((1, 2, 3, 4), 64)
    )
    weight_grad = jnp.sum(row_parts.astype(F32), axis=0)[:12, :96]
    dq, dk, dv = call(
        merge_kernel,
        (bf(ROWS, MODEL),) * 3,
        keep1, keep3, keep02, got13, pair_gather(send02),
        smem=False, hbm=5, hbm_out=(0, 1, 2),
        scratch=(vmem(ROWS, 4 * one), vmem(2, ROWS, two), vmem(3, ROWS, MODEL), dma(6)),
        flops=2_000_000_000,
    )
    return dq[None], dk[None], dv[None], weight_grad


def solution(mesh):
    rows = P("batch", "ctx", None)
    return jax.shard_map(
        local,
        mesh=mesh,
        in_specs=(rows, rows, rows, rows, P(), P()),
        out_specs=(rows, rows, rows, P("ctx", "batch")),
        check_vma=False,
    )
```

```python
import math

import jax
import jax.numpy as jnp
from jax import lax
from jax.experimental import pallas as pl
from jax.experimental.pallas import tpu as pltpu
from jax.sharding import PartitionSpec as P

LEVELS = 4
HEADS = 16
HEAD_WIDTH = 48
PAIR_WIDTH = 2 * HEAD_WIDTH
LEVEL_WIDTH = 4 * HEAD_WIDTH
LANES = 128
ROWS = 256
MODEL = 768
SENT = 448
SCALE = 1.0 / math.sqrt(HEAD_WIDTH)
BF = jnp.bfloat16
F32 = jnp.float32
VMEM_LIMIT = 24 * 1024 * 1024


def groups_over(bits, count):
    found = {}
    for index in range(count):
        rest = index
        for bit in bits:
            rest &= ~(1 << bit)
        found.setdefault(rest, []).append(index)
    return list(found.values())


def mm(a, b):
    return jnp.dot(a, b, preferred_element_type=F32)


def mm_nt(a, b):
    return lax.dot_general(a, b, (((1,), (1,)), ((), ())), preferred_element_type=F32)


def mm_tn(a, b):
    return lax.dot_general(a, b, (((0,), (0,)), ((), ())), preferred_element_type=F32)


def iota(shape, dim):
    return lax.broadcasted_iota(jnp.int32, shape, dim)


def one_hot(condition):
    return jnp.where(condition, 1.0, 0.0).astype(BF)


def turn(level, half):
    return (LEVEL_WIDTH * level + PAIR_WIDTH * half) & (LANES - 1)


def straight(shape, first):
    return (iota(shape, 1) - first) & (LANES - 1)


def first_head(shape, first):
    return straight(shape, first) < HEAD_WIDTH


def own_lanes(rows, head, first):
    lane = straight(rows.shape, first)
    return jnp.where((lane >= HEAD_WIDTH * head) & (lane < HEAD_WIDTH * (head + 1)), rows, jnp.zeros((), BF))


def start_all(pairs, sems, first=0):
    moves = [
        pltpu.make_async_copy(source, target, sems.at[first + index]) for index, (source, target) in enumerate(pairs)
    ]
    for move in moves:
        move.start()
    return moves


def wait_all(moves):
    for move in moves:
        move.wait()


def pack_kernel(
    off_hbm, q_hbm, k_hbm, v_hbm, c_hbm, w_hbm, tile_ref, mine_ref, other_ref, eight_ref,
    wide, q_ref, k_ref, v_ref, c_ref, w_ref, off_ref, sems,
):
    moves = start_all(
        ((off_hbm, off_ref), (c_hbm, c_ref), (w_hbm, w_ref), (q_hbm, q_ref), (k_hbm, k_ref), (v_hbm, v_ref)), sems
    )
    core = lax.axis_index("ctx") & 1
    moves[0].wait()
    for head in range(HEADS):
        tile_ref[head : head + 1, :] = jnp.full((1, LANES), off_ref[head], jnp.int32)
    hits = {}
    for half in range(2):
        for level in range(1, LEVELS):
            dilation = 1 << level
            count = ROWS // dilation
            target = iota((count, ROWS), 1) - dilation * iota((count, ROWS), 0)
            picked = [one_hot(target == (off_ref[4 * level + 2 * half + head] & (dilation - 1))) for head in range(2)]
            hits[half, level] = jnp.concatenate(picked, axis=0)

    def widen(place, rows):
        for half in range(2):
            for level in range(LEVELS):
                start = LEVEL_WIDTH * level + PAIR_WIDTH * half
                first = turn(level, half)
                block = rows[:, start - first : start - first + LANES]
                if first + PAIR_WIDTH > LANES:
                    later = rows[:, start - first + LANES : start - first + 2 * LANES]
                    block = jnp.where(iota(block.shape, 1) >= first, block, later)
                wide[half, level, :, LANES * place : LANES * (place + 1)] = block

    def select(lanes):
        for half in range(2):
            for level in range(1, LEVELS):
                count = ROWS >> level
                picked = mm(hits[half, level], wide[half, level, :, lanes])
                first = turn(level, half)
                chosen = jnp.where(first_head((count, picked.shape[1]), first), picked[:count], picked[count:])
                if level == 3:
                    for place in range(2):
                        part = pltpu.roll(chosen[:, LANES * place : LANES * (place + 1)], (-first) % LANES, 1)
                        part = part[:, :PAIR_WIDTH].astype(BF)
                        target = PAIR_WIDTH * (lanes.start // LANES + place)
                        eight_ref[half, :, target : target + PAIR_WIDTH] = part
                else:
                    chosen = chosen.astype(BF)
                    target = ROWS if level == 1 else 384

                    @pl.when(core == half)
                    def _(chosen=chosen, target=target, count=count):
                        mine_ref[target : target + count, lanes] = chosen

                    @pl.when(core != half)
                    def _(chosen=chosen, target=target, count=count):
                        other_ref[target : target + count, lanes] = chosen

    moves[1].wait()
    cotangent = c_ref[...]
    half_rows = ROWS // 2
    other_ref[SENT:704, :] = cotangent[:, :512]
    other_ref[704:832, 0:256] = cotangent[:half_rows, 512:]
    other_ref[704:832, 256:512] = cotangent[half_rows:, 512:]
    moves[2].wait()
    widen(0, mm_nt(cotangent, w_ref[...]).astype(BF))
    for place, rows_ref in ((1, q_ref), (2, k_ref), (3, v_ref)):
        moves[2 + place].wait()
        widen(place, rows_ref[...])
        if place != 2:
            select(slice(2 * LANES * (place // 2), 2 * LANES * (place // 2 + 1)))
    for half in range(2):
        for chip in range(1, 4):
            eight_ref[half + 2 * chip] = eight_ref[half]
    for half in range(2):

        @pl.when(core == half)
        def _(half=half):
            mine_ref[0:ROWS, :] = wide[half, 0]

        @pl.when(core != half)
        def _(half=half):
            other_ref[0:ROWS, :] = wide[half, 0]


def lanes_of(packed):
    return tuple(packed[:, LANES * index : LANES * (index + 1)] for index in (1, 2, 3, 0))


def attend(packed, first, queries=ROWS, weights_ref=None, low_ref=None, place=0):
    q, k, v, _ = lanes_of(packed)
    total = None
    for head in range(2):
        scores = mm_nt(q[:queries], own_lanes(k, head, first)) * SCALE
        raw = jnp.exp(scores - jnp.max(scores, axis=1, keepdims=True))
        weights = raw * (1.0 / jnp.sum(raw, axis=1, keepdims=True))
        low = weights.astype(BF)
        if weights_ref is not None:
            weights_ref[place + head] = weights
            low_ref[place + head] = low
        part = mm(low, own_lanes(v, head, first))
        total = part if total is None else total + part
    return total.astype(BF)


def attend_all(units, weights_ref, low_ref, scores_ref):
    done, dots = [], []
    for index, (packed, first) in enumerate(units):
        attended = attend(packed, first, ROWS, weights_ref, low_ref, 2 * index)
        grad = lanes_of(packed)[3]
        done.append(attended)
        for head in range(2):
            product = own_lanes(grad, head, first).astype(F32) * attended.astype(F32)
            dots.append(jnp.sum(product, axis=1, keepdims=True))
    for index, (packed, first) in enumerate(units):
        _, _, v, grad = lanes_of(packed)
        for head in range(2):
            place = 2 * index + head
            grad_weights = mm_nt(grad, own_lanes(v, head, first))
            scores_ref[place] = (weights_ref[place] * (grad_weights - dots[place])).astype(BF)
    grads = []
    for index, (packed, first) in enumerate(units):
        q, k, _, grad = lanes_of(packed)
        dq = dk = dv = None
        for head in range(2):
            place = 2 * index + head
            parts = (
                mm(scores_ref[place], own_lanes(k, head, first)),
                mm_tn(scores_ref[place], own_lanes(q, head, first)),
                mm_tn(low_ref[place], own_lanes(grad, head, first)),
            )
            dq, dk, dv = parts if head == 0 else (dq + parts[0], dk + parts[1], dv + parts[2])
        grads.append(jnp.concatenate([part.astype(BF) for part in (dq * SCALE, dk * SCALE, dv)], axis=1))
    return done, grads


def place_rows(tile_ref, rows, level, half, lane):
    dilation = 1 << level
    count = ROWS // dilation
    offsets = [tile_ref[pl.ds(4 * level + 2 * half + head, 1), :] & (dilation - 1) for head in range(2)]
    if level == 1:
        offset = jnp.concatenate(offsets, axis=1)
    else:
        offset = jnp.where(iota((1, LANES), 1) < count, offsets[0], offsets[1])[:, : 2 * count]
    shape = (ROWS, 2 * count)
    hits = one_hot(iota(shape, 0) - dilation * (iota(shape, 1) & (count - 1)) == offset)
    first = first_head(rows.shape, lane)
    zero = jnp.zeros((), BF)
    stacked = jnp.concatenate([jnp.where(first, rows, zero), jnp.where(first, zero, rows)], axis=0)
    return mm(hits, stacked).astype(BF)


def place_chip(tile_ref, mine, other, level, lane):
    core = lax.axis_index("ctx") & 1
    return jnp.concatenate([place_rows(tile_ref, rows, level, core, lane) for rows in (mine, other)], axis=0)


def fold_lanes(rows, level, first):
    shape = (LANES, LEVELS * PAIR_WIDTH)
    lane = (iota(shape, 0) - first) & (LANES - 1)
    return mm(rows, one_hot(iota(shape, 1) == jnp.where(lane < PAIR_WIDTH, lane + PAIR_WIDTH * level, -1)))


def first_kernel(
    tile_ref, mine_ref, other_ref, attended_ref, keep_hbm, send_hbm, grads_ref, weights_ref, low_ref, scores_ref, sems
):
    core = lax.axis_index("ctx") & 1
    zero_level = [attend(source[0:ROWS, :], turn(0, core)) for source in (mine_ref, other_ref)]
    packed = jnp.concatenate([mine_ref[ROWS:384, :], other_ref[ROWS:384, :]], axis=0)
    (done,), (grads,) = attend_all([(packed, turn(1, core))], weights_ref, low_ref, scores_ref)
    grads_ref[...] = grads
    half = ROWS // 2
    moves = start_all(((grads_ref.at[pl.ds(0, half)], keep_hbm), (grads_ref.at[pl.ds(half, half)], send_hbm)), sems)
    folded = fold_lanes(jnp.concatenate(zero_level, axis=0), 0, turn(0, core))
    folded += fold_lanes(place_chip(tile_ref, done[:half], done[half:], 1, turn(1, core)), 1, turn(1, core))
    attended_ref[...] = folded.astype(BF)
    wait_all(moves)


def second_kernel(
    tile_ref, eight_ref, old_ref, attended_ref, keep_ref, send_ref, done_ref, grads_ref, weights_ref, low_ref, scores_ref
):
    position = lax.axis_index("ctx")
    mine = pl.ds(pl.multiple_of(32 * (position & 7), 32), 32)
    other = pl.ds(pl.multiple_of(32 * ((position & 7) ^ 1), 32), 32)
    narrow = eight_ref[...].reshape(ROWS, 4 * PAIR_WIDTH)
    blank = jnp.zeros((ROWS, LANES - PAIR_WIDTH), BF)
    parts = []
    for place in range(4):
        parts += [narrow[:, PAIR_WIDTH * place : PAIR_WIDTH * (place + 1)], blank]
    (done,), (grads,) = attend_all([(jnp.concatenate(parts, axis=1), 0)], weights_ref, low_ref, scores_ref)
    done_ref[...] = done
    placed = place_chip(tile_ref, done_ref[mine, :], done_ref[other, :], 3, 0)
    attended_ref[...] = old_ref[...] + fold_lanes(placed, 3, 0).astype(BF)
    grads_ref[...] = grads
    keep_ref[...] = grads_ref[mine, :]
    send_ref[...] = grads_ref[other, :]


def weight_kernel(tile_ref, own_ref, other_ref, two_ref, got_two_ref, attended_ref, weight_ref):
    first = turn(2, lax.axis_index("ctx") & 1)
    done = attend(jnp.concatenate([two_ref[...], got_two_ref[...]], axis=0), first, ROWS // 2)
    placed = place_chip(tile_ref, done[:64], done[64:], 2, first)
    folded = attended_ref[...] + fold_lanes(placed, 2, first).astype(BF)
    narrow = jnp.concatenate([other_ref[704:832, 0:256], other_ref[704:832, 256:512]], axis=0)
    other = jnp.concatenate([other_ref[SENT:704, :], narrow], axis=1)
    part = mm_tn(jnp.concatenate([own_ref[...], other], axis=0), folded).astype(BF)
    for column in range(8):
        rows = part[96 * column : 96 * (column + 1)]
        weight_ref[2 * column, 0:96, :] = rows[:, 0:128]
        weight_ref[2 * column, 96:144, 0:64] = rows[0:48, 128:192]
        weight_ref[2 * column, 96:144, 64:128] = rows[48:96, 128:192]
        weight_ref[2 * column + 1, 0:96, :] = rows[:, 256:384]
        weight_ref[2 * column + 1, 96:144, 0:64] = rows[0:48, 192:256]
        weight_ref[2 * column + 1, 96:144, 64:128] = rows[48:96, 192:256]


def last_kernel(
    mine_ref, other_ref, two_ref, got_two_ref, send3_ref, keep_hbm, send_hbm, keep_ref, send_ref, weights_ref, low_ref, scores_ref, sems
):
    two = jnp.concatenate([two_ref[...], got_two_ref[...]], axis=0)
    core = lax.axis_index("ctx") & 1
    units = [(mine_ref[0:ROWS, :], turn(0, core)), (other_ref[0:ROWS, :], turn(0, core)), (two, turn(2, core))]
    _, grads = attend_all(units, weights_ref, low_ref, scores_ref)
    keep_ref[0:ROWS, :] = grads[0]
    send_ref[0:ROWS, :] = grads[1]
    keep_ref[ROWS:320, :] = grads[2][:64]
    send_ref[ROWS:320, :] = grads[2][64:128]
    send_ref[320:352, :] = send3_ref[...]
    wait_all(start_all(((keep_ref, keep_hbm), (send_ref, send_hbm)), sems))


def merge_kernel(
    tile_ref, keep3_ref, keep1_hbm, keep02_hbm, got1_hbm, got023_hbm, dq_hbm, dk_hbm, dv_hbm,
    keep1_ref, keep02_ref, got1_ref, got023_ref, full_ref, out_ref, sems,
):
    core = lax.axis_index("ctx") & 1
    moves = start_all(
        (
            (keep1_hbm, keep1_ref),
            (keep02_hbm, keep02_ref),
            (got1_hbm.at[1 - core], got1_ref),
            (got023_hbm.at[1 - core], got023_ref),
        ),
        sems,
    )
    wait_all(moves)
    for source, (one, two, three) in enumerate(
        (
            (keep1_ref[...], keep02_ref[ROWS:, :], keep3_ref[...]),
            (got1_ref[...], got023_ref[ROWS:320, :], got023_ref[320:, :]),
        )
    ):
        half = 1 - core if source else core
        slots = [three[:, LANES * array : LANES * (array + 1)].astype(F32) for array in range(3)]
        three = jnp.concatenate([pltpu.roll(slot, turn(3, half), 1) for slot in slots], axis=1).astype(BF)
        for level, rows in ((1, one), (2, two), (3, three)):
            full_ref[source, level - 1] = place_rows(tile_ref, rows, level, half, turn(level, half))
    out_moves = []
    lane = iota((ROWS, LANES), 1)
    for array, out_hbm in enumerate((dq_hbm, dk_hbm, dv_hbm)):
        lanes = slice(LANES * array, LANES * (array + 1))
        for own in range(2):

            @pl.when(core == own)
            def _(own=own, array=array, lanes=lanes):
                def piece(index):
                    level, half = index // 2, index % 2
                    if level:
                        return full_ref[int(half != own), level - 1, :, lanes]
                    return (keep02_ref if half == own else got023_ref)[0:ROWS, lanes]

                for block in range(MODEL // LANES):
                    index = LANES * block // PAIR_WIDTH
                    bound = PAIR_WIDTH * (index + 1) - LANES * block
                    out_ref[array, :, LANES * block : LANES * (block + 1)] = jnp.where(
                        lane < bound, piece(index), piece(index + 1)
                    )

        out_moves.append(pltpu.make_async_copy(out_ref.at[array], out_hbm, sems.at[array]))
        out_moves[-1].start()
    wait_all(out_moves)


def split_kernel(sums_ref, out_ref):
    position = lax.axis_index("ctx")
    core = position & 1
    upper = position >> 5
    shape = (256, LANES)
    row = iota(shape, 0)
    lane = iota(shape, 1)
    inner = row & 15
    source = 24 * (row >> 4) + 12 * core + inner
    second_level = (source >= LEVEL_WIDTH).astype(jnp.int32)
    rest = source - LEVEL_WIDTH * second_level
    second_half = rest >= PAIR_WIDTH
    column = PAIR_WIDTH * second_level + jnp.where(second_half, rest - PAIR_WIDTH, rest)
    wide_first = jnp.where(upper == 0, 0, 64)
    narrow_first = jnp.where(upper == 0, 128, 0)
    in_wide = (lane == column - wide_first) & (inner < 12)
    in_narrow = (lane == column - narrow_first) & (inner < 12)
    out = None
    for half in range(2):
        mine = second_half if half else ~second_half
        wide = one_hot(in_wide & mine)
        narrow = one_hot(in_narrow & mine & (lane < 64))
        sums = sums_ref[half]
        tail = sums[96:144]
        tail_rows = jnp.concatenate([tail, pltpu.roll(tail.astype(F32), 64, 1).astype(BF)], axis=0)
        part = mm_nt(wide, sums[0:96]) + mm_nt(narrow, tail_rows)
        out = part if out is None else out + part
    out_ref[:, 0:96] = out.astype(BF)
    out_ref[:, 96:128] = jnp.zeros((256, 32), BF)


def call(kernel, out_shape, *operands, hbm=0, hbm_out=(), scratch=(), flops=0):
    vmem = pl.BlockSpec(memory_space=pltpu.VMEM)
    far = pl.BlockSpec(memory_space=pltpu.HBM)
    near = len(operands) - hbm
    operands = operands[:near] + tuple(pltpu.with_memory_space_constraint(x, pltpu.HBM) for x in operands[near:])
    out_specs = vmem
    if isinstance(out_shape, tuple):
        out_shape, out_specs = list(out_shape), [vmem] * len(out_shape)
        for index in hbm_out:
            out_shape[index] = pltpu.HBM(out_shape[index].shape, out_shape[index].dtype)
            out_specs[index] = far
    return pl.pallas_call(
        kernel,
        out_shape=out_shape,
        in_specs=[vmem] * near + [far] * hbm,
        out_specs=out_specs,
        scratch_shapes=list(scratch),
        compiler_params=pltpu.CompilerParams(vmem_limit_bytes=VMEM_LIMIT),
        cost_estimate=pl.CostEstimate(flops=flops, bytes_accessed=0, transcendentals=0) if flops else None,
    )(*operands)


def pair_gather(block):
    return lax.all_gather(block, "ctx", axis=0, tiled=False, axis_index_groups=groups_over((0,), 64))


def swap(block, bit):
    return lax.ppermute(block, "ctx", [(index, index ^ (1 << bit)) for index in range(64)])


def local(queries, keys, values, cotangent, out_weight, offsets):
    def bf(*shape):
        return jax.ShapeDtypeStruct(shape, BF)

    def vmem(*shape):
        return pltpu.VMEM(shape, BF)

    def dma(count):
        return pltpu.SemaphoreType.DMA((count,))

    def steps(units):
        shape = (2 * units, ROWS, ROWS)
        return (pltpu.VMEM(shape, F32), vmem(*shape), vmem(*shape))

    wide = 3 * LANES
    rows = vmem(ROWS, MODEL)
    tile, mine, other, eight = call(
        pack_kernel,
        (jax.ShapeDtypeStruct((HEADS, LANES), jnp.int32), bf(SENT, 512), bf(832, 512), bf(8, 32, 384)),
        offsets, queries[0], keys[0], values[0], cotangent[0], out_weight,
        hbm=6,
        scratch=(
            vmem(2, LEVELS, ROWS, 4 * LANES), rows, rows, rows, rows, vmem(MODEL, MODEL),
            pltpu.SMEM((HEADS,), jnp.int32), dma(6),
        ),
    )
    eight = lax.all_to_all(eight, "ctx", 0, 0, tiled=True, axis_index_groups=groups_over((0, 1, 2), 64))
    other = swap(other, 0)
    own_two = jnp.concatenate([mine[384:SENT], other[384:SENT]], axis=0)
    got_two = swap(own_two, 1)
    attended, keep1, send1 = call(
        first_kernel,
        (bf(2 * ROWS, 384), bf(128, wide), bf(128, wide)),
        tile, mine, other,
        hbm_out=(1, 2), scratch=(vmem(ROWS, wide), *steps(1), dma(2)), flops=3_000_000_000,
    )
    attended, keep3, send3 = call(
        second_kernel,
        (bf(2 * ROWS, 384), bf(32, wide), bf(32, wide)),
        tile, eight, attended,
        scratch=(vmem(ROWS, LANES), vmem(ROWS, wide), *steps(1)), flops=3_000_000_000,
    )
    weight_parts = call(
        weight_kernel,
        bf(16, 144, 128),
        tile, cotangent[0], other, own_two, got_two, attended,
        flops=2_000_000_000,
    )
    weight_parts, mine, other, send1 = lax.optimization_barrier((weight_parts, mine, other, send1))
    plane = [[64 * batch + 32 * top + rest for batch in range(8) for top in range(2)] for rest in range(32)]
    column_parts = lax.all_to_all(weight_parts, ("batch", "ctx"), 0, 0, tiled=True, axis_index_groups=plane)
    keep02, send023 = call(
        last_kernel,
        (bf(320, wide), bf(352, wide)),
        mine, other, own_two, got_two, send3,
        hbm_out=(0, 1), scratch=(vmem(320, wide), vmem(352, wide), *steps(3), dma(2)), flops=5_000_000_000,
    )
    column_parts, got1 = lax.optimization_barrier((column_parts, pair_gather(send1)))
    column_sum = jnp.sum(column_parts.astype(F32), axis=0).astype(BF)
    row_parts = call(split_kernel, bf(256, 128), pair_gather(column_sum))
    row_parts, send023 = lax.optimization_barrier((row_parts, send023))
    row_parts = lax.all_to_all(
        row_parts.reshape(16, 16, 128), "ctx", 0, 0, tiled=True, axis_index_groups=groups_over((1, 2, 3, 4), 64)
    )
    weight_grad = jnp.sum(row_parts.astype(F32), axis=0)[:12, :96]
    dq, dk, dv = call(
        merge_kernel,
        (bf(ROWS, MODEL),) * 3,
        tile, keep3, keep1, keep02, got1, pair_gather(send023),
        hbm=4, hbm_out=(0, 1, 2),
        scratch=(
            vmem(128, wide), vmem(320, wide), vmem(128, wide), vmem(352, wide),
            vmem(2, 3, ROWS, wide), vmem(3, ROWS, MODEL), dma(4),
        ),
        flops=2_000_000_000,
    )
    return dq[None], dk[None], dv[None], weight_grad


def solution(mesh):
    rows = P("batch", "ctx", None)
    return jax.shard_map(
        local,
        mesh=mesh,
        in_specs=(rows, rows, rows, rows, P(), P()),
        out_specs=(rows, rows, rows, P("ctx", "batch")),
        check_vma=False,
    )
```

```python
import math

import jax
import jax.numpy as jnp
from jax import lax
from jax.experimental import pallas as pl
from jax.experimental.pallas import tpu as pltpu
from jax.sharding import PartitionSpec as P

LEVELS = 4
HEADS = 16
HEAD_WIDTH = 48
PAIR_WIDTH = 2 * HEAD_WIDTH
LEVEL_WIDTH = 4 * HEAD_WIDTH
LANES = 128
ROWS = 256
MODEL = 768
SENT = 448
NEAR_FIRST = 2
FAR_FIRST = 10
SCALE = 1.0 / math.sqrt(HEAD_WIDTH)
BF = jnp.bfloat16
F32 = jnp.float32
VMEM_LIMIT = 24 * 1024 * 1024


def groups_over(bits, count, first=0):
    found = {}
    for index in range(count):
        rest = index
        for bit in bits:
            rest &= ~(1 << bit)
        found.setdefault(rest, []).append(index)
    return [group[first:] + group[:first] for group in found.values()]


def mm(a, b):
    return jnp.dot(a, b, preferred_element_type=F32)


def mm_nt(a, b):
    return lax.dot_general(a, b, (((1,), (1,)), ((), ())), preferred_element_type=F32)


def mm_tn(a, b):
    return lax.dot_general(a, b, (((0,), (0,)), ((), ())), preferred_element_type=F32)


def iota(shape, dim):
    return lax.broadcasted_iota(jnp.int32, shape, dim)


def one_hot(condition):
    return jnp.where(condition, 1.0, 0.0).astype(BF)


def turn(level, half):
    return (LEVEL_WIDTH * level + PAIR_WIDTH * half) & (LANES - 1)


def straight(shape, first):
    return (iota(shape, 1) - first) & (LANES - 1)


def first_head(shape, first):
    return straight(shape, first) < HEAD_WIDTH


def own_lanes(rows, head, first):
    lane = straight(rows.shape, first)
    return jnp.where((lane >= HEAD_WIDTH * head) & (lane < HEAD_WIDTH * (head + 1)), rows, jnp.zeros((), BF))


def start_all(pairs, sems, first=0):
    moves = [
        pltpu.make_async_copy(source, target, sems.at[first + index]) for index, (source, target) in enumerate(pairs)
    ]
    for move in moves:
        move.start()
    return moves


def wait_all(moves):
    for move in moves:
        move.wait()


def pack_kernel(
    off_hbm, q_hbm, k_hbm, v_hbm, c_hbm, w_hbm, tile_ref, mine_ref, other_ref, eight_ref,
    wide, q_ref, k_ref, v_ref, c_ref, w_ref, off_ref, sems,
):
    moves = start_all(
        ((off_hbm, off_ref), (c_hbm, c_ref), (w_hbm, w_ref), (q_hbm, q_ref), (k_hbm, k_ref), (v_hbm, v_ref)), sems
    )
    core = lax.axis_index("ctx") & 1
    moves[0].wait()
    for head in range(HEADS):
        tile_ref[head : head + 1, :] = jnp.full((1, LANES), off_ref[head], jnp.int32)
    hits = {}
    for half in range(2):
        for level in range(1, LEVELS):
            dilation = 1 << level
            count = ROWS // dilation
            target = iota((count, ROWS), 1) - dilation * iota((count, ROWS), 0)
            picked = [one_hot(target == (off_ref[4 * level + 2 * half + head] & (dilation - 1))) for head in range(2)]
            hits[half, level] = jnp.concatenate(picked, axis=0)

    def widen(place, rows):
        for half in range(2):
            for level in range(LEVELS):
                start = LEVEL_WIDTH * level + PAIR_WIDTH * half
                first = turn(level, half)
                block = rows[:, start - first : start - first + LANES]
                if first + PAIR_WIDTH > LANES:
                    later = rows[:, start - first + LANES : start - first + 2 * LANES]
                    block = jnp.where(iota(block.shape, 1) >= first, block, later)
                wide[half, level, :, LANES * place : LANES * (place + 1)] = block

    turned = {}

    def select(lanes):
        for half in range(2):
            for level in range(1, LEVELS):
                count = ROWS >> level
                picked = mm(hits[half, level], wide[half, level, :, lanes])
                first = turn(level, half)
                chosen = jnp.where(first_head((count, picked.shape[1]), first), picked[:count], picked[count:])
                if level == 1:
                    chosen = chosen.astype(BF)

                    @pl.when(core == half)
                    def _(chosen=chosen):
                        mine_ref[ROWS:384, lanes] = chosen

                    @pl.when(core != half)
                    def _(chosen=chosen):
                        other_ref[ROWS:384, lanes] = chosen

                    continue
                for place in range(2):
                    slot = lanes.start // LANES + place
                    shift = (PAIR_WIDTH * slot - first) % LANES
                    part = chosen[:, LANES * place : LANES * (place + 1)]
                    turned[half, level, slot] = pltpu.roll(part, shift, 1) if shift else part

    def join():
        for half in range(2):
            for level in range(2, LEVELS):
                slots = [turned[half, level, slot] for slot in range(4)]
                lane = iota(slots[0].shape, 1)
                blocks = [
                    jnp.where(lane < PAIR_WIDTH - 32 * block, slots[block], slots[block + 1]).astype(BF)
                    for block in range(3)
                ]
                joined = jnp.concatenate(blocks, axis=1)
                if level == 3:
                    for chip in range(4):
                        eight_ref[half + 2 * chip] = joined
                else:

                    @pl.when(core == half)
                    def _(joined=joined):
                        mine_ref[384:SENT, 0:384] = joined

                    @pl.when(core != half)
                    def _(joined=joined):
                        other_ref[384:SENT, 0:384] = joined

    moves[1].wait()
    cotangent = c_ref[...]
    half_rows = ROWS // 2
    other_ref[SENT:704, :] = cotangent[:, :512]
    other_ref[704:832, 0:256] = cotangent[:half_rows, 512:]
    other_ref[704:832, 256:512] = cotangent[half_rows:, 512:]
    moves[2].wait()
    widen(0, mm_nt(cotangent, w_ref[...]).astype(BF))
    for place, rows_ref in ((1, q_ref), (2, k_ref), (3, v_ref)):
        moves[2 + place].wait()
        widen(place, rows_ref[...])
        if place != 2:
            select(slice(2 * LANES * (place // 2), 2 * LANES * (place // 2 + 1)))
    join()
    for half in range(2):

        @pl.when(core == half)
        def _(half=half):
            mine_ref[0:ROWS, :] = wide[half, 0]

        @pl.when(core != half)
        def _(half=half):
            other_ref[0:ROWS, :] = wide[half, 0]


def lanes_of(packed):
    return tuple(packed[:, LANES * index : LANES * (index + 1)] for index in (1, 2, 3, 0))


def spread_lanes(narrow):
    blank = jnp.zeros((narrow.shape[0], LANES - PAIR_WIDTH), BF)
    parts = []
    for place in range(4):
        parts += [narrow[:, PAIR_WIDTH * place : PAIR_WIDTH * (place + 1)], blank]
    return jnp.concatenate(parts, axis=1)


def attend(packed, first, queries=ROWS, weights_ref=None, low_ref=None, place=0):
    q, k, v, _ = lanes_of(packed)
    total = None
    for head in range(2):
        scores = mm_nt(q[:queries], own_lanes(k, head, first)) * SCALE
        raw = jnp.exp(scores - jnp.max(scores, axis=1, keepdims=True))
        weights = raw * (1.0 / jnp.sum(raw, axis=1, keepdims=True))
        low = weights.astype(BF)
        if weights_ref is not None:
            weights_ref[place + head] = weights
            low_ref[place + head] = low
        part = mm(low, own_lanes(v, head, first))
        total = part if total is None else total + part
    return total.astype(BF)


def attend_all(units, weights_ref, low_ref, scores_ref):
    done, dots = [], []
    for index, (packed, first) in enumerate(units):
        attended = attend(packed, first, ROWS, weights_ref, low_ref, 2 * index)
        grad = lanes_of(packed)[3]
        done.append(attended)
        for head in range(2):
            product = own_lanes(grad, head, first).astype(F32) * attended.astype(F32)
            dots.append(jnp.sum(product, axis=1, keepdims=True))
    for index, (packed, first) in enumerate(units):
        _, _, v, grad = lanes_of(packed)
        for head in range(2):
            place = 2 * index + head
            grad_weights = mm_nt(grad, own_lanes(v, head, first))
            scores_ref[place] = (weights_ref[place] * (grad_weights - dots[place])).astype(BF)
    grads = []
    for index, (packed, first) in enumerate(units):
        q, k, _, grad = lanes_of(packed)
        dq = dk = dv = None
        for head in range(2):
            place = 2 * index + head
            parts = (
                mm(scores_ref[place], own_lanes(k, head, first)),
                mm_tn(scores_ref[place], own_lanes(q, head, first)),
                mm_tn(low_ref[place], own_lanes(grad, head, first)),
            )
            dq, dk, dv = parts if head == 0 else (dq + parts[0], dk + parts[1], dv + parts[2])
        grads.append(jnp.concatenate([part.astype(BF) for part in (dq * SCALE, dk * SCALE, dv)], axis=1))
    return done, grads


def place_rows(tile_ref, rows, level, half, lane):
    dilation = 1 << level
    count = ROWS // dilation
    offsets = [tile_ref[pl.ds(4 * level + 2 * half + head, 1), :] & (dilation - 1) for head in range(2)]
    if level == 1:
        offset = jnp.concatenate(offsets, axis=1)
    else:
        offset = jnp.where(iota((1, LANES), 1) < count, offsets[0], offsets[1])[:, : 2 * count]
    shape = (ROWS, 2 * count)
    hits = one_hot(iota(shape, 0) - dilation * (iota(shape, 1) & (count - 1)) == offset)
    first = first_head(rows.shape, lane)
    zero = jnp.zeros((), BF)
    stacked = jnp.concatenate([jnp.where(first, rows, zero), jnp.where(first, zero, rows)], axis=0)
    return mm(hits, stacked).astype(BF)


def place_chip(tile_ref, mine, other, level, lane):
    core = lax.axis_index("ctx") & 1
    return jnp.concatenate([place_rows(tile_ref, rows, level, core, lane) for rows in (mine, other)], axis=0)


def fold_lanes(rows, level, first):
    shape = (LANES, LEVELS * PAIR_WIDTH)
    lane = (iota(shape, 0) - first) & (LANES - 1)
    return mm(rows, one_hot(iota(shape, 1) == jnp.where(lane < PAIR_WIDTH, lane + PAIR_WIDTH * level, -1)))


def first_kernel(
    tile_ref, mine_ref, other_ref, attended_ref, keep_hbm, send_hbm, grads_ref, weights_ref, low_ref, scores_ref, sems
):
    core = lax.axis_index("ctx") & 1
    zero_level = [attend(source[0:ROWS, :], turn(0, core)) for source in (mine_ref, other_ref)]
    packed = jnp.concatenate([mine_ref[ROWS:384, :], other_ref[ROWS:384, :]], axis=0)
    (done,), (grads,) = attend_all([(packed, turn(1, core))], weights_ref, low_ref, scores_ref)
    grads_ref[...] = grads
    half = ROWS // 2
    moves = start_all(((grads_ref.at[pl.ds(0, half)], keep_hbm), (grads_ref.at[pl.ds(half, half)], send_hbm)), sems)
    folded = fold_lanes(jnp.concatenate(zero_level, axis=0), 0, turn(0, core))
    folded += fold_lanes(place_chip(tile_ref, done[:half], done[half:], 1, turn(1, core)), 1, turn(1, core))
    attended_ref[...] = folded.astype(BF)
    wait_all(moves)


def second_kernel(
    tile_ref, eight_ref, old_ref, attended_ref, keep_ref, send_ref, done_ref, grads_ref, weights_ref, low_ref, scores_ref
):
    position = lax.axis_index("ctx")
    place = (position - NEAR_FIRST) & 7
    mine = pl.ds(pl.multiple_of(32 * place, 32), 32)
    other = pl.ds(pl.multiple_of(32 * (place ^ 1), 32), 32)
    packed = spread_lanes(eight_ref[...].reshape(ROWS, 4 * PAIR_WIDTH))
    (done,), (grads,) = attend_all([(packed, 0)], weights_ref, low_ref, scores_ref)
    done_ref[...] = done
    placed = place_chip(tile_ref, done_ref[mine, :], done_ref[other, :], 3, 0)
    attended_ref[...] = old_ref[...] + fold_lanes(placed, 3, 0).astype(BF)
    grads_ref[...] = grads
    keep_ref[...] = grads_ref[mine, :]
    send_ref[...] = grads_ref[other, :]


def weight_kernel(tile_ref, own_ref, other_ref, two_ref, got_two_ref, attended_ref, weight_hbm, weight_ref, sems):
    done = attend(spread_lanes(jnp.concatenate([two_ref[...], got_two_ref[...]], axis=0)), 0, ROWS // 2)
    placed = place_chip(tile_ref, done[:64], done[64:], 2, 0)
    folded = attended_ref[...] + fold_lanes(placed, 2, 0).astype(BF)
    narrow = jnp.concatenate([other_ref[704:832, 0:256], other_ref[704:832, 256:512]], axis=0)
    other = jnp.concatenate([other_ref[SENT:704, :], narrow], axis=1)
    cotangent = jnp.concatenate([own_ref[...], other], axis=0)
    moves = []
    for side in range(2):
        part = mm_tn(cotangent[:, 384 * side : 384 * (side + 1)], folded).astype(BF)
        for column in range(4):
            rows = part[96 * column : 96 * (column + 1)]
            place = 8 * side + 2 * column
            weight_ref[place, 0:96, :] = rows[:, 0:128]
            weight_ref[place, 96:144, 0:64] = rows[0:48, 128:192]
            weight_ref[place, 96:144, 64:128] = rows[48:96, 128:192]
            weight_ref[place + 1, 0:96, :] = rows[:, 256:384]
            weight_ref[place + 1, 96:144, 0:64] = rows[0:48, 192:256]
            weight_ref[place + 1, 96:144, 64:128] = rows[48:96, 192:256]
        blocks = pl.ds(8 * side, 8)
        moves += start_all(((weight_ref.at[blocks], weight_hbm.at[blocks]),), sems, side)
    wait_all(moves)


def last_kernel(
    mine_ref, other_ref, two_ref, got_two_ref, send3_ref, keep_hbm, send_hbm, keep_ref, send_ref, weights_ref, low_ref, scores_ref, sems
):
    two = spread_lanes(jnp.concatenate([two_ref[...], got_two_ref[...]], axis=0))
    core = lax.axis_index("ctx") & 1
    units = [(mine_ref[0:ROWS, :], turn(0, core)), (other_ref[0:ROWS, :], turn(0, core)), (two, 0)]
    _, grads = attend_all(units, weights_ref, low_ref, scores_ref)
    keep_ref[0:ROWS, :] = grads[0]
    send_ref[0:ROWS, :] = grads[1]
    keep_ref[ROWS:320, :] = grads[2][:64]
    send_ref[ROWS:320, :] = grads[2][64:128]
    send_ref[320:352, :] = send3_ref[...]
    wait_all(start_all(((keep_ref, keep_hbm), (send_ref, send_hbm)), sems))


def merge_kernel(
    tile_ref, keep3_ref, keep1_hbm, keep02_hbm, got1_hbm, got023_hbm, dq_hbm, dk_hbm, dv_hbm,
    keep1_ref, keep02_ref, got1_ref, got023_ref, full_ref, out_ref, sems,
):
    core = lax.axis_index("ctx") & 1
    moves = start_all(
        (
            (keep1_hbm, keep1_ref),
            (keep02_hbm, keep02_ref),
            (got1_hbm.at[1 - core], got1_ref),
            (got023_hbm.at[1 - core], got023_ref),
        ),
        sems,
    )
    wait_all(moves)
    for source, (one, two, three) in enumerate(
        (
            (keep1_ref[...], keep02_ref[ROWS:, :], keep3_ref[...]),
            (got1_ref[...], got023_ref[ROWS:320, :], got023_ref[320:, :]),
        )
    ):
        half = 1 - core if source else core
        for level, rows in ((1, one), (2, two), (3, three)):
            if level > 1:
                slots = [rows[:, LANES * array : LANES * (array + 1)].astype(F32) for array in range(3)]
                rows = jnp.concatenate([pltpu.roll(slot, turn(level, half), 1) for slot in slots], axis=1).astype(BF)
            full_ref[source, level - 1] = place_rows(tile_ref, rows, level, half, turn(level, half))
    out_moves = []
    lane = iota((ROWS, LANES), 1)
    for array, out_hbm in enumerate((dq_hbm, dk_hbm, dv_hbm)):
        lanes = slice(LANES * array, LANES * (array + 1))
        for own in range(2):

            @pl.when(core == own)
            def _(own=own, array=array, lanes=lanes):
                def piece(index):
                    level, half = index // 2, index % 2
                    if level:
                        return full_ref[int(half != own), level - 1, :, lanes]
                    return (keep02_ref if half == own else got023_ref)[0:ROWS, lanes]

                for block in range(MODEL // LANES):
                    index = LANES * block // PAIR_WIDTH
                    bound = PAIR_WIDTH * (index + 1) - LANES * block
                    out_ref[array, :, LANES * block : LANES * (block + 1)] = jnp.where(
                        lane < bound, piece(index), piece(index + 1)
                    )

        out_moves.append(pltpu.make_async_copy(out_ref.at[array], out_hbm, sems.at[array]))
        out_moves[-1].start()
    wait_all(out_moves)


def split_kernel(sums_ref, out_ref):
    position = lax.axis_index("ctx")
    core = position & 1
    upper = position >> 5
    shape = (256, LANES)
    row = iota(shape, 0)
    lane = iota(shape, 1)
    inner = row & 15
    source = 24 * (((row >> 4) + FAR_FIRST) & 15) + 12 * core + inner
    second_level = (source >= LEVEL_WIDTH).astype(jnp.int32)
    rest = source - LEVEL_WIDTH * second_level
    second_half = rest >= PAIR_WIDTH
    column = PAIR_WIDTH * second_level + jnp.where(second_half, rest - PAIR_WIDTH, rest)
    wide_first = jnp.where(upper == 0, 0, 64)
    narrow_first = jnp.where(upper == 0, 128, 0)
    in_wide = (lane == column - wide_first) & (inner < 12)
    in_narrow = (lane == column - narrow_first) & (inner < 12)
    out = None
    for half in range(2):
        mine = second_half if half else ~second_half
        wide = one_hot(in_wide & mine)
        narrow = one_hot(in_narrow & mine & (lane < 64))
        sums = sums_ref[half]
        tail = sums[96:144]
        tail_rows = jnp.concatenate([tail, pltpu.roll(tail.astype(F32), 64, 1).astype(BF)], axis=0)
        part = mm_nt(wide, sums[0:96]) + mm_nt(narrow, tail_rows)
        out = part if out is None else out + part
    out_ref[:, 0:96] = out.astype(BF)
    out_ref[:, 96:128] = jnp.zeros((256, 32), BF)


def call(kernel, out_shape, *operands, hbm=0, hbm_out=(), scratch=(), flops=0):
    vmem = pl.BlockSpec(memory_space=pltpu.VMEM)
    far = pl.BlockSpec(memory_space=pltpu.HBM)
    near = len(operands) - hbm
    operands = operands[:near] + tuple(pltpu.with_memory_space_constraint(x, pltpu.HBM) for x in operands[near:])
    out_specs = vmem
    if isinstance(out_shape, tuple):
        out_shape, out_specs = list(out_shape), [vmem] * len(out_shape)
        for index in hbm_out:
            out_shape[index] = pltpu.HBM(out_shape[index].shape, out_shape[index].dtype)
            out_specs[index] = far
    return pl.pallas_call(
        kernel,
        out_shape=out_shape,
        in_specs=[vmem] * near + [far] * hbm,
        out_specs=out_specs,
        scratch_shapes=list(scratch),
        compiler_params=pltpu.CompilerParams(vmem_limit_bytes=VMEM_LIMIT),
        cost_estimate=pl.CostEstimate(flops=flops, bytes_accessed=0, transcendentals=0) if flops else None,
    )(*operands)


def pair_gather(block):
    return lax.all_gather(block, "ctx", axis=0, tiled=False, axis_index_groups=groups_over((0,), 64))


def swap(block, bit):
    return lax.ppermute(block, "ctx", [(index, index ^ (1 << bit)) for index in range(64)])


def local(queries, keys, values, cotangent, out_weight, offsets):
    def bf(*shape):
        return jax.ShapeDtypeStruct(shape, BF)

    def vmem(*shape):
        return pltpu.VMEM(shape, BF)

    def dma(count):
        return pltpu.SemaphoreType.DMA((count,))

    def steps(units):
        shape = (2 * units, ROWS, ROWS)
        return (pltpu.VMEM(shape, F32), vmem(*shape), vmem(*shape))

    wide = 3 * LANES
    rows = vmem(ROWS, MODEL)
    tile, mine, other, eight = call(
        pack_kernel,
        (jax.ShapeDtypeStruct((HEADS, LANES), jnp.int32), bf(SENT, 512), bf(832, 512), bf(8, 32, 384)),
        offsets, queries[0], keys[0], values[0], cotangent[0], out_weight,
        hbm=6,
        scratch=(
            vmem(2, LEVELS, ROWS, 4 * LANES), rows, rows, rows, rows, vmem(MODEL, MODEL),
            pltpu.SMEM((HEADS,), jnp.int32), dma(6),
        ),
    )
    eight = lax.all_to_all(eight, "ctx", 0, 0, tiled=True, axis_index_groups=groups_over((0, 1, 2), 64, NEAR_FIRST))
    other = swap(other, 0)
    own_two = jnp.concatenate([mine[384:SENT, :384], other[384:SENT, :384]], axis=0)
    got_two = swap(own_two, 1)
    attended, keep1, send1 = call(
        first_kernel,
        (bf(2 * ROWS, 384), bf(128, wide), bf(128, wide)),
        tile, mine, other,
        hbm_out=(1, 2), scratch=(vmem(ROWS, wide), *steps(1), dma(2)), flops=3_000_000_000,
    )
    attended, keep3, send3 = call(
        second_kernel,
        (bf(2 * ROWS, 384), bf(32, wide), bf(32, wide)),
        tile, eight, attended,
        scratch=(vmem(ROWS, LANES), vmem(ROWS, wide), *steps(1)), flops=3_000_000_000,
    )
    (weight_parts,) = call(
        weight_kernel,
        (bf(16, 144, 128),),
        tile, cotangent[0], other, own_two, got_two, attended,
        hbm_out=(0,), scratch=(vmem(16, 144, 128), dma(2)), flops=2_000_000_000,
    )
    weight_parts, mine, other, send1 = lax.optimization_barrier((weight_parts, mine, other, send1))
    plane = [[64 * batch + 32 * top + rest for batch in range(8) for top in range(2)] for rest in range(32)]
    column_parts = lax.all_to_all(weight_parts, ("batch", "ctx"), 0, 0, tiled=True, axis_index_groups=plane)
    keep02, send023 = call(
        last_kernel,
        (bf(320, wide), bf(352, wide)),
        mine, other, own_two, got_two, send3,
        hbm_out=(0, 1), scratch=(vmem(320, wide), vmem(352, wide), *steps(3), dma(2)), flops=5_000_000_000,
    )
    column_parts, got1 = lax.optimization_barrier((column_parts, pair_gather(send1)))
    column_sum = jnp.sum(column_parts.astype(F32), axis=0).astype(BF)
    row_parts = call(split_kernel, bf(256, 128), pair_gather(column_sum))
    row_parts, send023 = lax.optimization_barrier((row_parts, send023))
    row_parts = lax.all_to_all(
        row_parts.reshape(16, 16, 128), "ctx", 0, 0, tiled=True, axis_index_groups=groups_over((1, 2, 3, 4), 64, FAR_FIRST)
    )
    weight_grad = jnp.sum(row_parts.astype(F32), axis=0)[:12, :96]
    dq, dk, dv = call(
        merge_kernel,
        (bf(ROWS, MODEL),) * 3,
        tile, keep3, keep1, keep02, got1, pair_gather(send023),
        hbm=4, hbm_out=(0, 1, 2),
        scratch=(
            vmem(128, wide), vmem(320, wide), vmem(128, wide), vmem(352, wide),
            vmem(2, 3, ROWS, wide), vmem(3, ROWS, MODEL), dma(4),
        ),
        flops=2_000_000_000,
    )
    return dq[None], dk[None], dv[None], weight_grad


def solution(mesh):
    rows = P("batch", "ctx", None)
    return jax.shard_map(
        local,
        mesh=mesh,
        in_specs=(rows, rows, rows, rows, P(), P()),
        out_specs=(rows, rows, rows, P("ctx", "batch")),
        check_vma=False,
    )
```

```python
import math

import jax
import jax.numpy as jnp
from jax import lax
from jax.experimental import pallas as pl
from jax.experimental.pallas import tpu as pltpu
from jax.sharding import PartitionSpec as P

LEVELS = 4
HEADS = 16
HEAD_WIDTH = 48
PAIR_WIDTH = 2 * HEAD_WIDTH
LEVEL_WIDTH = 4 * HEAD_WIDTH
LANES = 128
ROWS = 256
MODEL = 768
SENT = 448
NEAR_FIRST = 2
PLANE_FIRST = 9
FAR_FIRST = 10
SCALE = 1.0 / math.sqrt(HEAD_WIDTH)
BF = jnp.bfloat16
F32 = jnp.float32
VMEM_LIMIT = 24 * 1024 * 1024


def groups_over(bits, count, first=0):
    found = {}
    for index in range(count):
        rest = index
        for bit in bits:
            rest &= ~(1 << bit)
        found.setdefault(rest, []).append(index)
    return [group[first:] + group[:first] for group in found.values()]


def mm(a, b):
    return jnp.dot(a, b, preferred_element_type=F32)


def mm_nt(a, b):
    return lax.dot_general(a, b, (((1,), (1,)), ((), ())), preferred_element_type=F32)


def mm_tn(a, b):
    return lax.dot_general(a, b, (((0,), (0,)), ((), ())), preferred_element_type=F32)


def iota(shape, dim):
    return lax.broadcasted_iota(jnp.int32, shape, dim)


def one_hot(condition):
    return jnp.where(condition, 1.0, 0.0).astype(BF)


def turn(level, half):
    return (LEVEL_WIDTH * level + PAIR_WIDTH * half) & (LANES - 1)


def straight(shape, first):
    return (iota(shape, 1) - first) & (LANES - 1)


def first_head(shape, first):
    return straight(shape, first) < HEAD_WIDTH


def own_lanes(rows, head, first):
    lane = straight(rows.shape, first)
    return jnp.where((lane >= HEAD_WIDTH * head) & (lane < HEAD_WIDTH * (head + 1)), rows, jnp.zeros((), BF))


def start_all(pairs, sems, first=0):
    moves = [
        pltpu.make_async_copy(source, target, sems.at[first + index]) for index, (source, target) in enumerate(pairs)
    ]
    for move in moves:
        move.start()
    return moves


def wait_all(moves):
    for move in moves:
        move.wait()


def select_rows(wide, offsets, level, first):
    dilation = 1 << level
    count = ROWS // dilation
    target = iota((count, ROWS), 1) - dilation * iota((count, ROWS), 0)
    hits = [one_hot(target == (offset & (dilation - 1))) for offset in offsets]
    picked = mm(jnp.concatenate(hits, axis=0), wide)
    return jnp.where(first_head((count, picked.shape[1]), first), picked[:count], picked[count:])


def join_lanes(chosen, first):
    slots = [
        pltpu.roll(chosen[:, LANES * slot : LANES * (slot + 1)], (PAIR_WIDTH * slot - first) & (LANES - 1), 1)
        for slot in range(4)
    ]
    lane = iota(slots[0].shape, 1)
    blocks = [jnp.where(lane < PAIR_WIDTH - 32 * block, slots[block], slots[block + 1]) for block in range(3)]
    return jnp.concatenate([block.astype(BF) for block in blocks], axis=1)


def pack_kernel(
    off_hbm, q_hbm, k_hbm, v_hbm, c_hbm, w_hbm, tile_ref, wide_ref, eight_ref, last_ref,
    q_ref, k_ref, v_ref, c_ref, w_ref, off_ref, sems,
):
    moves = start_all(
        ((off_hbm, off_ref), (c_hbm, c_ref), (w_hbm, w_ref), (q_hbm, q_ref), (k_hbm, k_ref), (v_hbm, v_ref)), sems
    )

    def widen(place, rows):
        for half in range(2):
            for level in range(LEVELS):
                start = LEVEL_WIDTH * level + PAIR_WIDTH * half
                first = turn(level, half)
                block = rows[:, start - first : start - first + LANES]
                if first + PAIR_WIDTH > LANES:
                    later = rows[:, start - first + LANES : start - first + 2 * LANES]
                    block = jnp.where(iota(block.shape, 1) >= first, block, later)
                lanes = slice(LANES * place, LANES * (place + 1))
                if level == 3:
                    last_ref[half, :, lanes] = block
                else:
                    wide_ref[half, level, :, lanes] = block

    moves[0].wait()
    for head in range(HEADS):
        tile_ref[head : head + 1, :] = jnp.full((1, LANES), off_ref[head], jnp.int32)
    moves[1].wait()
    moves[2].wait()
    widen(0, mm_nt(c_ref[...], w_ref[...]).astype(BF))
    for place, rows_ref in ((1, q_ref), (2, k_ref), (3, v_ref)):
        moves[2 + place].wait()
        widen(place, rows_ref[...])
    for half in range(2):
        offsets = [off_ref[12 + 2 * half + head] for head in range(2)]
        first = turn(3, half)
        joined = join_lanes(select_rows(last_ref[half], offsets, 3, first), first)
        for chip in range(4):
            eight_ref[half + 2 * chip] = joined


def share_kernel(tile_ref, wide_ref, c_ref, mine_ref, other_ref):
    core = lax.axis_index("ctx") & 1
    for target_ref, half in ((mine_ref, core), (other_ref, 1 - core)):
        target_ref[0:ROWS, :] = wide_ref[half, 0]
        for level in (1, 2):
            offsets = [tile_ref[pl.ds(4 * level + 2 * half + head, 1), 0:1] for head in range(2)]
            first = turn(level, half)
            chosen = select_rows(wide_ref[half, level], offsets, level, first)
            if level == 1:
                target_ref[ROWS:384, :] = chosen.astype(BF)
            else:
                target_ref[384:SENT, 0:384] = join_lanes(chosen, first)
    cotangent = c_ref[...]
    half_rows = ROWS // 2
    other_ref[SENT:704, :] = cotangent[:, :512]
    other_ref[704:832, 0:256] = cotangent[:half_rows, 512:]
    other_ref[704:832, 256:512] = cotangent[half_rows:, 512:]


def lanes_of(packed):
    return tuple(packed[:, LANES * index : LANES * (index + 1)] for index in (1, 2, 3, 0))


def spread_lanes(narrow):
    blank = jnp.zeros((narrow.shape[0], LANES - PAIR_WIDTH), BF)
    parts = []
    for place in range(4):
        parts += [narrow[:, PAIR_WIDTH * place : PAIR_WIDTH * (place + 1)], blank]
    return jnp.concatenate(parts, axis=1)


def attend(packed, first, queries=ROWS, weights_ref=None, low_ref=None, place=0):
    q, k, v, _ = lanes_of(packed)
    total = None
    for head in range(2):
        scores = mm_nt(q[:queries], own_lanes(k, head, first)) * SCALE
        raw = jnp.exp(scores - jnp.max(scores, axis=1, keepdims=True))
        weights = raw * (1.0 / jnp.sum(raw, axis=1, keepdims=True))
        low = weights.astype(BF)
        if weights_ref is not None:
            weights_ref[place + head] = weights
            low_ref[place + head] = low
        part = mm(low, own_lanes(v, head, first))
        total = part if total is None else total + part
    return total.astype(BF)


def attend_all(units, weights_ref, low_ref, scores_ref):
    done, dots = [], []
    for index, (packed, first) in enumerate(units):
        attended = attend(packed, first, ROWS, weights_ref, low_ref, 2 * index)
        grad = lanes_of(packed)[3]
        done.append(attended)
        for head in range(2):
            product = own_lanes(grad, head, first).astype(F32) * attended.astype(F32)
            dots.append(jnp.sum(product, axis=1, keepdims=True))
    for index, (packed, first) in enumerate(units):
        _, _, v, grad = lanes_of(packed)
        for head in range(2):
            place = 2 * index + head
            grad_weights = mm_nt(grad, own_lanes(v, head, first))
            scores_ref[place] = (weights_ref[place] * (grad_weights - dots[place])).astype(BF)
    grads = []
    for index, (packed, first) in enumerate(units):
        q, k, _, grad = lanes_of(packed)
        dq = dk = dv = None
        for head in range(2):
            place = 2 * index + head
            parts = (
                mm(scores_ref[place], own_lanes(k, head, first)),
                mm_tn(scores_ref[place], own_lanes(q, head, first)),
                mm_tn(low_ref[place], own_lanes(grad, head, first)),
            )
            dq, dk, dv = parts if head == 0 else (dq + parts[0], dk + parts[1], dv + parts[2])
        grads.append(jnp.concatenate([part.astype(BF) for part in (dq * SCALE, dk * SCALE, dv)], axis=1))
    return done, grads


def place_rows(tile_ref, rows, level, half, lane):
    dilation = 1 << level
    count = ROWS // dilation
    offsets = [tile_ref[pl.ds(4 * level + 2 * half + head, 1), :] & (dilation - 1) for head in range(2)]
    if level == 1:
        offset = jnp.concatenate(offsets, axis=1)
    else:
        offset = jnp.where(iota((1, LANES), 1) < count, offsets[0], offsets[1])[:, : 2 * count]
    shape = (ROWS, 2 * count)
    hits = one_hot(iota(shape, 0) - dilation * (iota(shape, 1) & (count - 1)) == offset)
    first = first_head(rows.shape, lane)
    zero = jnp.zeros((), BF)
    stacked = jnp.concatenate([jnp.where(first, rows, zero), jnp.where(first, zero, rows)], axis=0)
    return mm(hits, stacked).astype(BF)


def place_chip(tile_ref, mine, other, level, lane):
    core = lax.axis_index("ctx") & 1
    return jnp.concatenate([place_rows(tile_ref, rows, level, core, lane) for rows in (mine, other)], axis=0)


def fold_lanes(rows, level, first):
    shape = (LANES, LEVELS * PAIR_WIDTH)
    lane = (iota(shape, 0) - first) & (LANES - 1)
    return mm(rows, one_hot(iota(shape, 1) == jnp.where(lane < PAIR_WIDTH, lane + PAIR_WIDTH * level, -1)))


def level_one(mine_ref, other_ref):
    return jnp.concatenate([mine_ref[ROWS:384, :], other_ref[ROWS:384, :]], axis=0)


def first_kernel(tile_ref, mine_ref, other_ref, attended_ref):
    core = lax.axis_index("ctx") & 1
    zero_level = [attend(source[0:ROWS, :], turn(0, core)) for source in (mine_ref, other_ref)]
    done = attend(level_one(mine_ref, other_ref), turn(1, core))
    half = ROWS // 2
    folded = fold_lanes(jnp.concatenate(zero_level, axis=0), 0, turn(0, core))
    folded += fold_lanes(place_chip(tile_ref, done[:half], done[half:], 1, turn(1, core)), 1, turn(1, core))
    attended_ref[...] = folded.astype(BF)


def own_rows_of_eight():
    place = (lax.axis_index("ctx") - NEAR_FIRST) & 7
    return pl.ds(pl.multiple_of(32 * place, 32), 32), pl.ds(pl.multiple_of(32 * (place ^ 1), 32), 32)


def second_kernel(tile_ref, eight_ref, old_ref, attended_ref, done_ref):
    mine, other = own_rows_of_eight()
    done_ref[...] = attend(spread_lanes(eight_ref[...].reshape(ROWS, 4 * PAIR_WIDTH)), 0)
    placed = place_chip(tile_ref, done_ref[mine, :], done_ref[other, :], 3, 0)
    attended_ref[...] = old_ref[...] + fold_lanes(placed, 3, 0).astype(BF)


def weight_kernel(tile_ref, own_ref, other_ref, two_ref, got_two_ref, attended_ref, weight_ref):
    done = attend(spread_lanes(jnp.concatenate([two_ref[...], got_two_ref[...]], axis=0)), 0, ROWS // 2)
    placed = place_chip(tile_ref, done[:64], done[64:], 2, 0)
    folded = attended_ref[...] + fold_lanes(placed, 2, 0).astype(BF)
    narrow = jnp.concatenate([other_ref[704:832, 0:256], other_ref[704:832, 256:512]], axis=0)
    other = jnp.concatenate([other_ref[SENT:704, :], narrow], axis=1)
    cotangent = jnp.concatenate([own_ref[...], other], axis=0)
    part = mm_tn(cotangent, folded).astype(BF)
    for block in range(16):
        rows = part[96 * (block // 2) : 96 * (block // 2 + 1)]
        place = (block - PLANE_FIRST) % 16
        wide, narrow = (256, 192) if block % 2 else (0, 128)
        weight_ref[place, 0:96, :] = rows[:, wide : wide + 128]
        weight_ref[place, 96:144, 0:64] = rows[0:48, narrow : narrow + 64]
        weight_ref[place, 96:144, 64:128] = rows[48:96, narrow : narrow + 64]


def last_kernel(
    mine_ref, other_ref, two_ref, got_two_ref, eight_ref, keep_hbm, send_ref,
    keep_ref, grads_ref, weights_ref, low_ref, scores_ref, sems,
):
    core = lax.axis_index("ctx") & 1
    two = spread_lanes(jnp.concatenate([two_ref[...], got_two_ref[...]], axis=0))
    units = [
        (mine_ref[0:ROWS, :], turn(0, core)),
        (other_ref[0:ROWS, :], turn(0, core)),
        (level_one(mine_ref, other_ref), turn(1, core)),
        (two, 0),
        (spread_lanes(eight_ref[...].reshape(ROWS, 4 * PAIR_WIDTH)), 0),
    ]
    _, grads = attend_all(units, weights_ref, low_ref, scores_ref)
    grads_ref[...] = grads[4]
    for index, (target_ref, rows) in enumerate(zip((keep_ref, send_ref), own_rows_of_eight())):
        target_ref[0:ROWS, :] = grads[index]
        target_ref[ROWS:384, :] = grads[2][128 * index : 128 * (index + 1)]
        target_ref[384:448, :] = grads[3][64 * index : 64 * (index + 1)]
        target_ref[448:480, :] = grads_ref[rows, :]
    wait_all(start_all(((keep_ref, keep_hbm),), sems))


def merge_kernel(
    tile_ref, keep_hbm, got_hbm, dq_hbm, dk_hbm, dv_hbm, keep_ref, got_ref, full_ref, out_ref, sems
):
    core = lax.axis_index("ctx") & 1
    wait_all(start_all(((keep_hbm, keep_ref), (got_hbm.at[1 - core], got_ref)), sems))
    for source, source_ref in enumerate((keep_ref, got_ref)):
        half = 1 - core if source else core
        for level, rows in ((1, source_ref[ROWS:384, :]), (2, source_ref[384:448, :]), (3, source_ref[448:480, :])):
            if level > 1:
                slots = [rows[:, LANES * array : LANES * (array + 1)].astype(F32) for array in range(3)]
                rows = jnp.concatenate([pltpu.roll(slot, turn(level, half), 1) for slot in slots], axis=1).astype(BF)
            full_ref[source, level - 1] = place_rows(tile_ref, rows, level, half, turn(level, half))
    out_moves = []
    lane = iota((ROWS, LANES), 1)
    for array, out_hbm in enumerate((dq_hbm, dk_hbm, dv_hbm)):
        lanes = slice(LANES * array, LANES * (array + 1))
        for own in range(2):

            @pl.when(core == own)
            def _(own=own, array=array, lanes=lanes):
                def piece(index):
                    level, half = index // 2, index % 2
                    if level:
                        return full_ref[int(half != own), level - 1, :, lanes]
                    return (keep_ref if half == own else got_ref)[0:ROWS, lanes]

                for block in range(MODEL // LANES):
                    index = LANES * block // PAIR_WIDTH
                    bound = PAIR_WIDTH * (index + 1) - LANES * block
                    out_ref[array, :, LANES * block : LANES * (block + 1)] = jnp.where(
                        lane < bound, piece(index), piece(index + 1)
                    )

        out_moves.append(pltpu.make_async_copy(out_ref.at[array], out_hbm, sems.at[array]))
        out_moves[-1].start()
    wait_all(out_moves)


def split_kernel(sums_ref, out_ref):
    position = lax.axis_index("ctx")
    core = position & 1
    upper = position >> 5
    shape = (256, LANES)
    row = iota(shape, 0)
    lane = iota(shape, 1)
    inner = row & 15
    source = 24 * (((row >> 4) + FAR_FIRST) & 15) + 12 * core + inner
    second_level = (source >= LEVEL_WIDTH).astype(jnp.int32)
    rest = source - LEVEL_WIDTH * second_level
    second_half = rest >= PAIR_WIDTH
    column = PAIR_WIDTH * second_level + jnp.where(second_half, rest - PAIR_WIDTH, rest)
    wide_first = jnp.where(upper == 0, 0, 64)
    narrow_first = jnp.where(upper == 0, 128, 0)
    in_wide = (lane == column - wide_first) & (inner < 12)
    in_narrow = (lane == column - narrow_first) & (inner < 12)
    out = None
    for half in range(2):
        mine = second_half if half else ~second_half
        wide = one_hot(in_wide & mine)
        narrow = one_hot(in_narrow & mine & (lane < 64))
        sums = sums_ref[half]
        tail = sums[96:144]
        tail_rows = jnp.concatenate([tail, pltpu.roll(tail.astype(F32), 64, 1).astype(BF)], axis=0)
        part = mm_nt(wide, sums[0:96]) + mm_nt(narrow, tail_rows)
        out = part if out is None else out + part
    out_ref[:, 0:96] = out.astype(BF)
    out_ref[:, 96:128] = jnp.zeros((256, 32), BF)


def call(kernel, out_shape, *operands, hbm=0, hbm_out=(), scratch=(), flops=0):
    vmem = pl.BlockSpec(memory_space=pltpu.VMEM)
    far = pl.BlockSpec(memory_space=pltpu.HBM)
    near = len(operands) - hbm
    operands = operands[:near] + tuple(pltpu.with_memory_space_constraint(x, pltpu.HBM) for x in operands[near:])
    out_specs = vmem
    if isinstance(out_shape, tuple):
        out_shape, out_specs = list(out_shape), [vmem] * len(out_shape)
        for index in hbm_out:
            out_shape[index] = pltpu.HBM(out_shape[index].shape, out_shape[index].dtype)
            out_specs[index] = far
    return pl.pallas_call(
        kernel,
        out_shape=out_shape,
        in_specs=[vmem] * near + [far] * hbm,
        out_specs=out_specs,
        scratch_shapes=list(scratch),
        compiler_params=pltpu.CompilerParams(vmem_limit_bytes=VMEM_LIMIT),
        cost_estimate=pl.CostEstimate(flops=flops, bytes_accessed=0, transcendentals=0) if flops else None,
    )(*operands)


def pair_gather(block):
    return lax.all_gather(block, "ctx", axis=0, tiled=False, axis_index_groups=groups_over((0,), 64))


def swap(block, bit):
    return lax.ppermute(block, "ctx", [(index, index ^ (1 << bit)) for index in range(64)])


def local(queries, keys, values, cotangent, out_weight, offsets):
    def bf(*shape):
        return jax.ShapeDtypeStruct(shape, BF)

    def vmem(*shape):
        return pltpu.VMEM(shape, BF)

    def dma(count):
        return pltpu.SemaphoreType.DMA((count,))

    def steps(units):
        shape = (2 * units, ROWS, ROWS)
        return (pltpu.VMEM(shape, F32), vmem(*shape), vmem(*shape))

    wide = 3 * LANES
    rows = vmem(ROWS, MODEL)
    tile, wide_rows, eight = call(
        pack_kernel,
        (jax.ShapeDtypeStruct((HEADS, LANES), jnp.int32), bf(2, 3, ROWS, 512), bf(8, 32, 384)),
        offsets, queries[0], keys[0], values[0], cotangent[0], out_weight,
        hbm=6,
        scratch=(
            vmem(2, ROWS, 512), rows, rows, rows, rows, vmem(MODEL, MODEL), pltpu.SMEM((HEADS,), jnp.int32), dma(6)
        ),
    )
    eight = lax.all_to_all(
        eight, "ctx", 0, 0, tiled=True, axis_index_groups=groups_over((0, 1, 2), 64, NEAR_FIRST)
    )
    mine, other = call(share_kernel, (bf(SENT, 512), bf(832, 512)), tile, wide_rows, cotangent[0], flops=1_000_000)
    other = swap(other, 0)
    own_two = jnp.concatenate([mine[384:SENT, :384], other[384:SENT, :384]], axis=0)
    got_two = swap(own_two, 1)
    attended = call(first_kernel, bf(2 * ROWS, 384), tile, mine, other, flops=1_000_000)
    attended = call(
        second_kernel, bf(2 * ROWS, 384), tile, eight, attended, scratch=(vmem(ROWS, LANES),), flops=1_000_000_000
    )
    weight_parts = call(
        weight_kernel,
        bf(16, 144, 128),
        tile, cotangent[0], other, own_two, got_two, attended,
        flops=2_000_000_000,
    )
    weight_parts, mine, other = lax.optimization_barrier((weight_parts, mine, other))
    members = [(place + PLANE_FIRST) % 16 for place in range(16)]
    plane = [[64 * (member // 2) + 32 * (member % 2) + rest for member in members] for rest in range(32)]
    column_parts = lax.all_to_all(weight_parts, ("batch", "ctx"), 0, 0, tiled=True, axis_index_groups=plane)
    keep, send = call(
        last_kernel,
        (bf(480, wide), bf(480, wide)),
        mine, other, own_two, got_two, eight,
        hbm_out=(0,), scratch=(vmem(480, wide), vmem(ROWS, wide), *steps(5), dma(1)),
        flops=8_000_000_000,
    )
    column_sum = jnp.sum(column_parts.astype(F32), axis=0).astype(BF)
    row_parts = call(split_kernel, bf(256, 128), pair_gather(column_sum))
    row_parts, send = lax.optimization_barrier((row_parts, send))
    row_parts = lax.all_to_all(
        row_parts.reshape(16, 16, 128), "ctx", 0, 0, tiled=True, axis_index_groups=groups_over((1, 2, 3, 4), 64, FAR_FIRST)
    )
    weight_grad = jnp.sum(row_parts.astype(F32), axis=0)[:12, :96]
    dq, dk, dv = call(
        merge_kernel,
        (bf(ROWS, MODEL),) * 3,
        tile, keep, pair_gather(send),
        hbm=2, hbm_out=(0, 1, 2),
        scratch=(vmem(480, wide), vmem(480, wide), vmem(2, 3, ROWS, wide), vmem(3, ROWS, MODEL), dma(3)),
        flops=2_000_000_000,
    )
    return dq[None], dk[None], dv[None], weight_grad


def solution(mesh):
    rows = P("batch", "ctx", None)
    return jax.shard_map(
        local,
        mesh=mesh,
        in_specs=(rows, rows, rows, rows, P(), P()),
        out_specs=(rows, rows, rows, P("ctx", "batch")),
        check_vma=False,
    )
```

```python
import math

import jax
import jax.numpy as jnp
from jax import lax
from jax.experimental import pallas as pl
from jax.experimental.pallas import tpu as pltpu
from jax.sharding import PartitionSpec as P

LEVELS = 4
HEADS = 16
HEAD_WIDTH = 48
PAIR_WIDTH = 2 * HEAD_WIDTH
LEVEL_WIDTH = 4 * HEAD_WIDTH
LANES = 128
ROWS = 256
MODEL = 768
SENT = 448
NEAR_FIRST = 2
PLANE_FIRST = 9
FAR_FIRST = 10
SCALE = 1.0 / math.sqrt(HEAD_WIDTH)
BF = jnp.bfloat16
F32 = jnp.float32
VMEM_LIMIT = 24 * 1024 * 1024


def groups_over(bits, count, first=0):
    found = {}
    for index in range(count):
        rest = index
        for bit in bits:
            rest &= ~(1 << bit)
        found.setdefault(rest, []).append(index)
    return [group[first:] + group[:first] for group in found.values()]


def mm(a, b):
    return jnp.dot(a, b, preferred_element_type=F32)


def mm_nt(a, b):
    return lax.dot_general(a, b, (((1,), (1,)), ((), ())), preferred_element_type=F32)


def mm_tn(a, b):
    return lax.dot_general(a, b, (((0,), (0,)), ((), ())), preferred_element_type=F32)


def iota(shape, dim):
    return lax.broadcasted_iota(jnp.int32, shape, dim)


def one_hot(condition):
    return jnp.where(condition, 1.0, 0.0).astype(BF)


def turn(level, half):
    return (LEVEL_WIDTH * level + PAIR_WIDTH * half) & (LANES - 1)


def straight(shape, first):
    return (iota(shape, 1) - first) & (LANES - 1)


def first_head(shape, first):
    return straight(shape, first) < HEAD_WIDTH


def own_lanes(rows, head, first):
    lane = straight(rows.shape, first)
    return jnp.where((lane >= HEAD_WIDTH * head) & (lane < HEAD_WIDTH * (head + 1)), rows, jnp.zeros((), BF))


def start_all(pairs, sems, first=0):
    moves = [
        pltpu.make_async_copy(source, target, sems.at[first + index]) for index, (source, target) in enumerate(pairs)
    ]
    for move in moves:
        move.start()
    return moves


def wait_all(moves):
    for move in moves:
        move.wait()


def select_rows(wide, offsets, level, first):
    dilation = 1 << level
    count = ROWS // dilation
    target = iota((count, ROWS), 1) - dilation * iota((count, ROWS), 0)
    hits = [one_hot(target == (offset & (dilation - 1))) for offset in offsets]
    picked = mm(jnp.concatenate(hits, axis=0), wide)
    return jnp.where(first_head((count, picked.shape[1]), first), picked[:count], picked[count:])


def join_lanes(chosen, first):
    slots = [
        pltpu.roll(chosen[:, LANES * slot : LANES * (slot + 1)], (PAIR_WIDTH * slot - first) & (LANES - 1), 1)
        for slot in range(4)
    ]
    lane = iota(slots[0].shape, 1)
    blocks = [jnp.where(lane < PAIR_WIDTH - 32 * block, slots[block], slots[block + 1]) for block in range(3)]
    return jnp.concatenate([block.astype(BF) for block in blocks], axis=1)


def pack_kernel(
    off_hbm, q_hbm, k_hbm, v_hbm, c_hbm, w_hbm, tile_ref, wide_ref, eight_ref, last_ref,
    q_ref, k_ref, v_ref, c_ref, w_ref, off_ref, sems,
):
    moves = start_all(
        ((off_hbm, off_ref), (c_hbm, c_ref), (w_hbm, w_ref), (q_hbm, q_ref), (k_hbm, k_ref), (v_hbm, v_ref)), sems
    )

    def widen(place, rows):
        for half in range(2):
            for level in range(LEVELS):
                start = LEVEL_WIDTH * level + PAIR_WIDTH * half
                first = turn(level, half)
                block = rows[:, start - first : start - first + LANES]
                if first + PAIR_WIDTH > LANES:
                    later = rows[:, start - first + LANES : start - first + 2 * LANES]
                    block = jnp.where(iota(block.shape, 1) >= first, block, later)
                lanes = slice(LANES * place, LANES * (place + 1))
                if level == 3:
                    last_ref[half, :, lanes] = block
                else:
                    wide_ref[half, level, :, lanes] = block

    moves[0].wait()
    for head in range(HEADS):
        tile_ref[head : head + 1, :] = jnp.full((1, LANES), off_ref[head], jnp.int32)
    moves[1].wait()
    moves[2].wait()
    widen(0, mm_nt(c_ref[...], w_ref[...]).astype(BF))
    for place, rows_ref in ((1, q_ref), (2, k_ref), (3, v_ref)):
        moves[2 + place].wait()
        widen(place, rows_ref[...])
    for half in range(2):
        offsets = [off_ref[12 + 2 * half + head] for head in range(2)]
        first = turn(3, half)
        joined = join_lanes(select_rows(last_ref[half], offsets, 3, first), first)
        for chip in range(4):
            eight_ref[half + 2 * chip] = joined


def share_kernel(tile_ref, wide_ref, c_ref, mine_ref, other_ref):
    core = lax.axis_index("ctx") & 1
    for target_ref, half in ((mine_ref, core), (other_ref, 1 - core)):
        target_ref[0:ROWS, :] = wide_ref[half, 0]
        for level in (1, 2):
            offsets = [tile_ref[pl.ds(4 * level + 2 * half + head, 1), 0:1] for head in range(2)]
            first = turn(level, half)
            chosen = select_rows(wide_ref[half, level], offsets, level, first)
            if level == 1:
                target_ref[ROWS:384, :] = chosen.astype(BF)
            else:
                target_ref[384:SENT, 0:384] = join_lanes(chosen, first)
    cotangent = c_ref[...]
    half_rows = ROWS // 2
    other_ref[SENT:704, :] = cotangent[:, :512]
    other_ref[704:832, 0:256] = cotangent[:half_rows, 512:]
    other_ref[704:832, 256:512] = cotangent[half_rows:, 512:]


def lanes_of(packed):
    return tuple(packed[:, LANES * index : LANES * (index + 1)] for index in (1, 2, 3, 0))


def spread_lanes(narrow):
    blank = jnp.zeros((narrow.shape[0], LANES - PAIR_WIDTH), BF)
    parts = []
    for place in range(4):
        parts += [narrow[:, PAIR_WIDTH * place : PAIR_WIDTH * (place + 1)], blank]
    return jnp.concatenate(parts, axis=1)


def attend(packed, first, queries=ROWS, weights_ref=None, low_ref=None, place=0):
    q, k, v, _ = lanes_of(packed)
    total = None
    for head in range(2):
        scores = mm_nt(q[:queries], own_lanes(k, head, first)) * SCALE
        raw = jnp.exp(scores - jnp.max(scores, axis=1, keepdims=True))
        weights = raw * (1.0 / jnp.sum(raw, axis=1, keepdims=True))
        low = weights.astype(BF)
        if weights_ref is not None:
            weights_ref[place + head] = weights
            low_ref[place + head] = low
        part = mm(low, own_lanes(v, head, first))
        total = part if total is None else total + part
    return total.astype(BF)


def attend_all(units, weights_ref, low_ref, scores_ref):
    done, dots = [], []
    for index, (packed, first) in enumerate(units):
        attended = attend(packed, first, ROWS, weights_ref, low_ref, 2 * index)
        grad = lanes_of(packed)[3]
        done.append(attended)
        for head in range(2):
            product = own_lanes(grad, head, first).astype(F32) * attended.astype(F32)
            dots.append(jnp.sum(product, axis=1, keepdims=True))
    for index, (packed, first) in enumerate(units):
        _, _, v, grad = lanes_of(packed)
        for head in range(2):
            place = 2 * index + head
            grad_weights = mm_nt(grad, own_lanes(v, head, first))
            scores_ref[place] = (weights_ref[place] * (grad_weights - dots[place])).astype(BF)
    grads = []
    for index, (packed, first) in enumerate(units):
        q, k, _, grad = lanes_of(packed)
        dq = dk = dv = None
        for head in range(2):
            place = 2 * index + head
            parts = (
                mm(scores_ref[place], own_lanes(k, head, first)),
                mm_tn(scores_ref[place], own_lanes(q, head, first)),
                mm_tn(low_ref[place], own_lanes(grad, head, first)),
            )
            dq, dk, dv = parts if head == 0 else (dq + parts[0], dk + parts[1], dv + parts[2])
        grads.append(jnp.concatenate([part.astype(BF) for part in (dq * SCALE, dk * SCALE, dv)], axis=1))
    return done, grads


def place_rows(tile_ref, rows, level, half, lane):
    dilation = 1 << level
    count = ROWS // dilation
    offsets = [tile_ref[pl.ds(4 * level + 2 * half + head, 1), :] & (dilation - 1) for head in range(2)]
    if level == 1:
        offset = jnp.concatenate(offsets, axis=1)
    else:
        offset = jnp.where(iota((1, LANES), 1) < count, offsets[0], offsets[1])[:, : 2 * count]
    shape = (ROWS, 2 * count)
    hits = one_hot(iota(shape, 0) - dilation * (iota(shape, 1) & (count - 1)) == offset)
    first = first_head(rows.shape, lane)
    zero = jnp.zeros((), BF)
    stacked = jnp.concatenate([jnp.where(first, rows, zero), jnp.where(first, zero, rows)], axis=0)
    return mm(hits, stacked).astype(BF)


def place_chip(tile_ref, mine, other, level, lane):
    core = lax.axis_index("ctx") & 1
    return jnp.concatenate([place_rows(tile_ref, rows, level, core, lane) for rows in (mine, other)], axis=0)


def fold_lanes(rows, level, first):
    shape = (LANES, LEVELS * PAIR_WIDTH)
    lane = (iota(shape, 0) - first) & (LANES - 1)
    return mm(rows, one_hot(iota(shape, 1) == jnp.where(lane < PAIR_WIDTH, lane + PAIR_WIDTH * level, -1)))


def level_one(mine_ref, other_ref):
    return jnp.concatenate([mine_ref[ROWS:384, :], other_ref[ROWS:384, :]], axis=0)


def first_kernel(tile_ref, mine_ref, other_ref, attended_ref):
    core = lax.axis_index("ctx") & 1
    zero_level = [attend(source[0:ROWS, :], turn(0, core)) for source in (mine_ref, other_ref)]
    done = attend(level_one(mine_ref, other_ref), turn(1, core))
    half = ROWS // 2
    folded = fold_lanes(jnp.concatenate(zero_level, axis=0), 0, turn(0, core))
    folded += fold_lanes(place_chip(tile_ref, done[:half], done[half:], 1, turn(1, core)), 1, turn(1, core))
    attended_ref[...] = folded.astype(BF)


def own_rows_of_eight():
    place = (lax.axis_index("ctx") - NEAR_FIRST) & 7
    return pl.ds(pl.multiple_of(32 * place, 32), 32), pl.ds(pl.multiple_of(32 * (place ^ 1), 32), 32)


def second_kernel(tile_ref, eight_ref, old_ref, attended_ref, done_ref):
    mine, other = own_rows_of_eight()
    done_ref[...] = attend(spread_lanes(eight_ref[...].reshape(ROWS, 4 * PAIR_WIDTH)), 0)
    placed = place_chip(tile_ref, done_ref[mine, :], done_ref[other, :], 3, 0)
    attended_ref[...] = old_ref[...] + fold_lanes(placed, 3, 0).astype(BF)


def weight_kernel(tile_ref, own_ref, other_ref, two_ref, got_two_ref, attended_ref, weight_ref):
    done = attend(spread_lanes(jnp.concatenate([two_ref[...], got_two_ref[...]], axis=0)), 0, ROWS // 2)
    placed = place_chip(tile_ref, done[:64], done[64:], 2, 0)
    folded = attended_ref[...] + fold_lanes(placed, 2, 0).astype(BF)
    narrow = jnp.concatenate([other_ref[704:832, 0:256], other_ref[704:832, 256:512]], axis=0)
    other = jnp.concatenate([other_ref[SENT:704, :], narrow], axis=1)
    cotangent = jnp.concatenate([own_ref[...], other], axis=0)
    part = mm_tn(cotangent, folded).astype(BF)
    for block in range(16):
        rows = part[96 * (block // 2) : 96 * (block // 2 + 1)]
        place = (block - PLANE_FIRST) % 16
        wide, narrow = (256, 192) if block % 2 else (0, 128)
        weight_ref[place, 0:96, :] = rows[:, wide : wide + 128]
        weight_ref[place, 96:144, 0:64] = rows[0:48, narrow : narrow + 64]
        weight_ref[place, 96:144, 64:128] = rows[48:96, narrow : narrow + 64]


def last_kernel(
    mine_ref, other_ref, two_ref, got_two_ref, eight_ref, keep_hbm, send_ref,
    keep_ref, grads_ref, weights_ref, low_ref, scores_ref, sems,
):
    core = lax.axis_index("ctx") & 1
    two = spread_lanes(jnp.concatenate([two_ref[...], got_two_ref[...]], axis=0))
    units = [
        (mine_ref[0:ROWS, :], turn(0, core)),
        (other_ref[0:ROWS, :], turn(0, core)),
        (level_one(mine_ref, other_ref), turn(1, core)),
        (two, 0),
        (spread_lanes(eight_ref[...].reshape(ROWS, 4 * PAIR_WIDTH)), 0),
    ]
    _, grads = attend_all(units, weights_ref, low_ref, scores_ref)
    grads_ref[...] = grads[4]
    for index, (target_ref, rows) in enumerate(zip((keep_ref, send_ref), own_rows_of_eight())):
        target_ref[0:ROWS, :] = grads[index]
        target_ref[ROWS:384, :] = grads[2][128 * index : 128 * (index + 1)]
        target_ref[384:448, :] = grads[3][64 * index : 64 * (index + 1)]
        target_ref[448:480, :] = grads_ref[rows, :]
    wait_all(start_all(((keep_ref, keep_hbm),), sems))


def merge_kernel(
    tile_ref, keep_hbm, got_hbm, dq_hbm, dk_hbm, dv_hbm, keep_ref, got_ref, full_ref, out_ref, sems
):
    core = lax.axis_index("ctx") & 1
    wait_all(start_all(((keep_hbm, keep_ref), (got_hbm.at[1 - core], got_ref)), sems))
    for source, source_ref in enumerate((keep_ref, got_ref)):
        half = 1 - core if source else core
        for level, rows in ((1, source_ref[ROWS:384, :]), (2, source_ref[384:448, :]), (3, source_ref[448:480, :])):
            if level > 1:
                slots = [rows[:, LANES * array : LANES * (array + 1)].astype(F32) for array in range(3)]
                rows = jnp.concatenate([pltpu.roll(slot, turn(level, half), 1) for slot in slots], axis=1).astype(BF)
            full_ref[source, level - 1] = place_rows(tile_ref, rows, level, half, turn(level, half))
    out_moves = []
    lane = iota((ROWS, LANES), 1)
    for array, out_hbm in enumerate((dq_hbm, dk_hbm, dv_hbm)):
        lanes = slice(LANES * array, LANES * (array + 1))
        for own in range(2):

            @pl.when(core == own)
            def _(own=own, array=array, lanes=lanes):
                def piece(index):
                    level, half = index // 2, index % 2
                    if level:
                        return full_ref[int(half != own), level - 1, :, lanes]
                    return (keep_ref if half == own else got_ref)[0:ROWS, lanes]

                for block in range(MODEL // LANES):
                    index = LANES * block // PAIR_WIDTH
                    bound = PAIR_WIDTH * (index + 1) - LANES * block
                    out_ref[array, :, LANES * block : LANES * (block + 1)] = jnp.where(
                        lane < bound, piece(index), piece(index + 1)
                    )

        out_moves.append(pltpu.make_async_copy(out_ref.at[array], out_hbm, sems.at[array]))
        out_moves[-1].start()
    wait_all(out_moves)


def split_kernel(sums_ref, out_ref):
    position = lax.axis_index("ctx")
    core = position & 1
    upper = position >> 5
    shape = (256, LANES)
    row = iota(shape, 0)
    lane = iota(shape, 1)
    inner = row & 15
    source = 24 * (((row >> 4) + FAR_FIRST) & 15) + 12 * core + inner
    second_level = (source >= LEVEL_WIDTH).astype(jnp.int32)
    rest = source - LEVEL_WIDTH * second_level
    second_half = rest >= PAIR_WIDTH
    column = PAIR_WIDTH * second_level + jnp.where(second_half, rest - PAIR_WIDTH, rest)
    wide_first = jnp.where(upper == 0, 0, 64)
    narrow_first = jnp.where(upper == 0, 128, 0)
    in_wide = (lane == column - wide_first) & (inner < 12)
    in_narrow = (lane == column - narrow_first) & (inner < 12)
    out = None
    for half in range(2):
        mine = second_half if half else ~second_half
        wide = one_hot(in_wide & mine)
        narrow = one_hot(in_narrow & mine & (lane < 64))
        sums = sums_ref[half]
        tail = sums[96:144]
        tail_rows = jnp.concatenate([tail, pltpu.roll(tail.astype(F32), 64, 1).astype(BF)], axis=0)
        part = mm_nt(wide, sums[0:96]) + mm_nt(narrow, tail_rows)
        out = part if out is None else out + part
    out = jnp.concatenate([out, jnp.zeros((256, 32), F32)], axis=1)
    for chip in range(16):
        rows = [out[16 * chip + 4 * third : 16 * chip + 4 * (third + 1)] for third in range(3)]
        out_ref[chip] = jnp.concatenate(rows, axis=1).astype(BF)


def total_kernel(parts_ref, out_ref):
    total = jnp.sum(parts_ref[...].astype(F32), axis=0)
    for third in range(3):
        out_ref[4 * third : 4 * (third + 1), :] = total[:, LANES * third : LANES * third + PAIR_WIDTH]


def call(kernel, out_shape, *operands, hbm=0, hbm_out=(), scratch=(), flops=0):
    vmem = pl.BlockSpec(memory_space=pltpu.VMEM)
    far = pl.BlockSpec(memory_space=pltpu.HBM)
    near = len(operands) - hbm
    operands = operands[:near] + tuple(pltpu.with_memory_space_constraint(x, pltpu.HBM) for x in operands[near:])
    out_specs = vmem
    if isinstance(out_shape, tuple):
        out_shape, out_specs = list(out_shape), [vmem] * len(out_shape)
        for index in hbm_out:
            out_shape[index] = pltpu.HBM(out_shape[index].shape, out_shape[index].dtype)
            out_specs[index] = far
    return pl.pallas_call(
        kernel,
        out_shape=out_shape,
        in_specs=[vmem] * near + [far] * hbm,
        out_specs=out_specs,
        scratch_shapes=list(scratch),
        compiler_params=pltpu.CompilerParams(vmem_limit_bytes=VMEM_LIMIT),
        cost_estimate=pl.CostEstimate(flops=flops, bytes_accessed=0, transcendentals=0) if flops else None,
    )(*operands)


def pair_gather(block):
    return lax.all_gather(block, "ctx", axis=0, tiled=False, axis_index_groups=groups_over((0,), 64))


def swap(block, bit):
    return lax.ppermute(block, "ctx", [(index, index ^ (1 << bit)) for index in range(64)])


def local(queries, keys, values, cotangent, out_weight, offsets):
    def bf(*shape):
        return jax.ShapeDtypeStruct(shape, BF)

    def vmem(*shape):
        return pltpu.VMEM(shape, BF)

    def dma(count):
        return pltpu.SemaphoreType.DMA((count,))

    def steps(units):
        shape = (2 * units, ROWS, ROWS)
        return (pltpu.VMEM(shape, F32), vmem(*shape), vmem(*shape))

    wide = 3 * LANES
    rows = vmem(ROWS, MODEL)
    tile, wide_rows, eight = call(
        pack_kernel,
        (jax.ShapeDtypeStruct((HEADS, LANES), jnp.int32), bf(2, 3, ROWS, 512), bf(8, 32, 384)),
        offsets, queries[0], keys[0], values[0], cotangent[0], out_weight,
        hbm=6,
        scratch=(
            vmem(2, ROWS, 512), rows, rows, rows, rows, vmem(MODEL, MODEL), pltpu.SMEM((HEADS,), jnp.int32), dma(6)
        ),
    )
    eight = lax.all_to_all(
        eight, "ctx", 0, 0, tiled=True, axis_index_groups=groups_over((0, 1, 2), 64, NEAR_FIRST)
    )
    mine, other = call(share_kernel, (bf(SENT, 512), bf(832, 512)), tile, wide_rows, cotangent[0], flops=1_000_000)
    other = swap(other, 0)
    own_two = jnp.concatenate([mine[384:SENT, :384], other[384:SENT, :384]], axis=0)
    got_two = swap(own_two, 1)
    attended = call(first_kernel, bf(2 * ROWS, 384), tile, mine, other, flops=1_000_000)
    attended = call(
        second_kernel, bf(2 * ROWS, 384), tile, eight, attended, scratch=(vmem(ROWS, LANES),), flops=1_000_000_000
    )
    weight_parts = call(
        weight_kernel,
        bf(16, 144, 128),
        tile, cotangent[0], other, own_two, got_two, attended,
        flops=2_000_000_000,
    )
    weight_parts, mine, other = lax.optimization_barrier((weight_parts, mine, other))
    members = [(place + PLANE_FIRST) % 16 for place in range(16)]
    plane = [[64 * (member // 2) + 32 * (member % 2) + rest for member in members] for rest in range(32)]
    column_parts = lax.all_to_all(weight_parts, ("batch", "ctx"), 0, 0, tiled=True, axis_index_groups=plane)
    keep, send = call(
        last_kernel,
        (bf(480, wide), bf(480, wide)),
        mine, other, own_two, got_two, eight,
        hbm_out=(0,), scratch=(vmem(480, wide), vmem(ROWS, wide), *steps(5), dma(1)),
        flops=8_000_000_000,
    )
    column_sum = jnp.sum(column_parts.astype(F32), axis=0).astype(BF)
    row_parts = call(split_kernel, bf(16, 4, 384), pair_gather(column_sum))
    row_parts, send = lax.optimization_barrier((row_parts, send))
    row_parts = lax.all_to_all(
        row_parts, "ctx", 0, 0, tiled=True, axis_index_groups=groups_over((1, 2, 3, 4), 64, FAR_FIRST)
    )
    weight_grad = call(total_kernel, jax.ShapeDtypeStruct((12, 96), F32), row_parts)
    dq, dk, dv = call(
        merge_kernel,
        (bf(ROWS, MODEL),) * 3,
        tile, keep, pair_gather(send),
        hbm=2, hbm_out=(0, 1, 2),
        scratch=(vmem(480, wide), vmem(480, wide), vmem(2, 3, ROWS, wide), vmem(3, ROWS, MODEL), dma(3)),
        flops=2_000_000_000,
    )
    return dq[None], dk[None], dv[None], weight_grad


def solution(mesh):
    rows = P("batch", "ctx", None)
    return jax.shard_map(
        local,
        mesh=mesh,
        in_specs=(rows, rows, rows, rows, P(), P()),
        out_specs=(rows, rows, rows, P("ctx", "batch")),
        check_vma=False,
    )
```
